128 devices in a mesh: lon: 16 (over x, y), lat: 8 (over z, core).
Axes of the slice: x: 4, y: 4, z: 4, core: 2. Of those that a mesh axis runs over, the one named last changes fastest.
Arguments:
- checkpoint: float32 [8, 512, 9600], P('lat', 'lon'), may hold values from -6 to 6
- slot_dest: int32 [8, 512], P('lat'), may hold values from -1 to 511, as said below
- kmt: int32 [1280, 7680], P('lat', 'lon'), may hold values from 0 to 2, as said below
- kappa: float32 [2, 1280, 7680], P(None, 'lat', 'lon'), may hold values from 0.02 to 0.2
Outputs:
- new_tracer: float32 [2, 2, 1280, 7680], P(None, None, 'lat', 'lon')
- stream: float32 [1280, 7680], P('lat', 'lon')
The draws below stay inside these ranges and needn't reach their ends.
Inputs may be any that keep to these rules, and one draw needn't show every extreme that they name: `slot_dest`: in each band every value e * 32 + p is named by at most one slot; at most 2 slots of one checkpoint owner's 32 slots name one new owner e, and exactly 2 for some pair in every band. Positions that no slot names are land blocks. kmt is 0 on every point of a land block.
All inputs are finite; a program needn't handle non-finite values.
Results may differ from the reference program's by a relative error of at most 0.0001.
Values sent between devices are 32-bit elements; how exact they have to be, the bound alone decides.
A program may use at most 128 MiB of HBM per device.

```python
import math
import jax
import jax.numpy as jnp

BH = 40
BW = 60
LEV = 2
BX = 8
BY = 4
ITERS = 3
Q = 32
PAYN = 9600
GY = 1280
GX = 7680
N_LON = 16
N_LAT = 8


def ocean_layout(key):
    base = jax.random.fold_in(key, 11)
    capacity = Q // N_LON

    def one_band(band_key):
        keys = jax.random.split(band_key, 4)
        spots = jax.vmap(lambda k: jax.random.permutation(k, Q))(jax.random.split(keys[0], N_LON))
        slots = jax.vmap(lambda k: jax.random.permutation(k, Q))(jax.random.split(keys[1], N_LON))
        offset = jax.random.randint(keys[2], (), 1, N_LON)
        shape = (N_LON, N_LON, capacity)
        source = jnp.broadcast_to(jnp.arange(N_LON, dtype=jnp.int32)[:, None, None], shape)
        target = jnp.broadcast_to(jnp.arange(N_LON, dtype=jnp.int32)[None, :, None], shape)
        copy_id = jnp.broadcast_to(jnp.arange(capacity, dtype=jnp.int32)[None, None, :], shape)
        draw_ten = jax.random.randint(keys[3], shape, 0, 10)
        ocean = (draw_ten < 7) | (source == (target + offset) % N_LON)
        position = spots[target, source * capacity + copy_id]
        slot = slots[source, target * capacity + copy_id]
        value = jnp.where(ocean, target * Q + position, -1)
        dest = jnp.zeros((N_LON, Q), jnp.int32).at[source, slot].set(value)
        present = jnp.zeros((N_LON, Q), jnp.int32).at[target, position].set(ocean.astype(jnp.int32))
        return (dest.reshape(N_LON * Q), present)
    return jax.vmap(one_band)(jax.random.split(base, N_LAT))


def draw_slot_dest(key, part):
    dest, present = ocean_layout(key)
    return dest.astype(jnp.int32)


def draw_kmt(key, part):
    dest, present = ocean_layout(key)
    blockmap = present.reshape(N_LAT, N_LON, BY, BX).transpose(0, 2, 1, 3).reshape(N_LAT * BY, N_LON * BX)
    cells = jnp.repeat(jnp.repeat(blockmap, BH, axis=0), BW, axis=1)
    draw_many = jax.random.randint(jax.random.fold_in(key, 23), (GY, GX), 0, 16)
    levels = jnp.where(draw_many < 2, 0, 1 + draw_many % LEV)
    return (cells * levels).astype(jnp.int32)


def steps_of(key, shape, shards, least, top_value):
    factor_of = 1.0
    for dim, blocks in shards:
        heights = jax.random.uniform(jax.random.fold_in(jax.random.fold_in(key, 6), dim), (blocks,), jnp.float32, least / len(shards), top_value / len(shards))
        factor_of = factor_of * jnp.repeat(jnp.exp(heights), shape[dim] // blocks).reshape((-1,) + (1,) * (len(shape) - 1 - dim))
    return factor_of


def scatter_about(key, dims, deviation, limit, cuts=(), kind=jnp.bfloat16):
    array = jax.random.normal(key, dims, jnp.float32) * deviation
    if len(cuts) > 0:
        array = steps_of(key, dims, cuts, -0.22, 0.18) * array
    return jnp.clip(array, min=-limit, max=limit).astype(kind)


def setup_inputs(seed: int = 0) -> dict:
    seeds = jax.random.split(jax.random.key(seed), 5)
    return {
        "checkpoint": scatter_about(seeds[0], (N_LAT, N_LON * Q, PAYN), 1.0, 6.0, ((0, 8), (1, 16)), jnp.float32),
        "slot_dest": draw_slot_dest(jax.random.fold_in(seeds[4], 71), 0),
        "kmt": draw_kmt(jax.random.fold_in(seeds[4], 71), 0),
        "kappa": jnp.clip(jnp.exp(math.log(0.2) - 2.3025851 * jax.random.uniform(seeds[3], (LEV, GY, GX), jnp.float32) ** steps_of(seeds[3], (LEV, GY, GX), ((1, 8), (2, 16)), -0.2, 0.2)), 0.02, 0.2),
    }


thermal = 0.25
haline = 0.75
cabbeling = 0.05


def widen(field):
    beside_all = jnp.concatenate([field[..., -1:], field, field[..., :1]], axis=-1)
    pad_width = [(0, 0)] * (field.ndim - 2) + [(1, 1), (0, 0)]
    return jnp.pad(beside_all, pad_width)


def operate(vector, depth, column):
    wide = widen(vector)
    edges = wide[2:, 1:-1] + wide[:-2, 1:-1] + wide[1:-1, 2:] + wide[1:-1, :-2]
    corners = wide[2:, 2:] + wide[2:, :-2] + wide[:-2, 2:] + wide[:-2, :-2]
    return column * ((6.0 + depth) * vector - edges - 0.5 * corners)


def reference(checkpoint, slot_dest, kmt, kappa):
    total = N_LAT * N_LON * Q
    band = jnp.arange(N_LAT, dtype=jnp.int32)[:, None]
    target = jnp.where(slot_dest >= 0, band * (N_LON * Q) + slot_dest, total).astype(jnp.int32)
    blocks = checkpoint.reshape(total, PAYN)
    placed = jnp.zeros((total + 1, PAYN), jnp.float32).at[target.reshape(-1)].set(blocks)[:total]
    field = placed.reshape(N_LAT, N_LON, BY, BX, 2, LEV, BH, BW)
    field = field.transpose(4, 5, 0, 2, 6, 1, 3, 7).reshape(2, LEV, GY, GX)
    levels = jnp.arange(LEV, dtype=jnp.int32)
    wet = (levels[:, None, None] < kmt[None]).astype(jnp.float32)
    tracer = field * wet
    tracer_w = widen(tracer)
    wet_w = widen(wet)
    kappa_w = widen(kappa)
    tracer_c = tracer_w[..., 1:-1, 1:-1]
    wet_c = wet_w[:, 1:-1, 1:-1]
    kappa_c = kappa_w[:, 1:-1, 1:-1]
    change = jnp.zeros_like(tracer)
    for dy, dx in ((0, 1), (0, -1), (1, 0), (-1, 0)):
        rows = slice(1 + dy, 1 + dy + GY)
        cols = slice(1 + dx, 1 + dx + GX)
        face = 0.5 * (kappa_c + kappa_w[:, rows, cols]) * wet_c * wet_w[:, rows, cols]
        change = change + face * (tracer_w[..., rows, cols] - tracer_c)
    new_tracer = wet * (tracer + change)
    dz = 1.0 + 0.5 * jnp.arange(LEV, dtype=jnp.float32)
    temp = new_tracer[0]
    salt = new_tracer[1]
    density = wet * (haline * salt - thermal * temp - cabbeling * temp * temp)
    forcing = jnp.sum(dz[:, None, None] * density, axis=0)
    depth = jnp.sum(dz[:, None, None] * wet, axis=0)
    column = (kmt > 0).astype(jnp.float32)
    stream = jnp.zeros_like(forcing)
    residual = column * forcing
    direction = residual
    norm_now = jnp.sum(residual * residual)
    for step in range(ITERS):
        image = operate(direction, depth, column)
        alpha = norm_now / jnp.sum(direction * image)
        stream = stream + alpha * direction
        residual = residual - alpha * image
        norm_next = jnp.sum(residual * residual)
        direction = residual + (norm_next / norm_now) * direction
        norm_now = norm_next
    return new_tracer, stream
```

```python
import jax
import jax.numpy as jnp
from jax import lax
from jax.experimental import pallas as pl
from jax.experimental.pallas import tpu as pltpu
from jax.sharding import PartitionSpec as P

BW = 60
BH = 40
BX = 8
BY = 4
Q = 32
ROWS = 160
COLS = 480
NLON = 16
NLAT = 8
SIDE = 4
TILES = 21
SHIFT = 6.0
CHUNK = 1920

thermal = 0.25
haline = 0.75
cabbeling = 0.05

f32 = jnp.float32


def owners(dest, me):
    dest = dest.reshape(NLON, Q)
    own = dest >> 5
    slot = jnp.arange(Q, dtype=jnp.int32)
    mine = lax.dynamic_index_in_dim(own, me, 0, keepdims=False)
    goes = mine[None] == jnp.arange(NLON, dtype=jnp.int32)[:, None]
    one = jnp.min(jnp.where(goes, slot, Q - 1), axis=1)
    two = jnp.max(jnp.where(goes, slot, 0), axis=1)
    first = jnp.min(jnp.where(own == me, slot, Q), axis=1, keepdims=True)
    code = 2 * jnp.arange(NLON, dtype=jnp.int32)[:, None] + (slot != first).astype(jnp.int32)
    here = dest[None] == me * Q + slot[:, None, None]
    found = jnp.max(jnp.where(here, code[None], 0), axis=(1, 2))
    return jnp.concatenate([one, two, found >> 1, found & 1])


def rows_of(i):
    return pl.ds(pl.multiple_of(i * 8, 8), 8)


def kernel(table, ckpt, kmt, kappa, out_t, out_s,
           blocks, parted, packed, landed, levels, kap, tr, hk,
           east_o, west_o, north_o, south_o, east_i, west_i, north_i, south_i, corner_i,
           vs, col, dep, fresh_t, stream, part, red1, red2,
           in_sem, out_sem, a2a_s, a2a_r, halo_s, halo_r, red_s, red_r):
    lon = lax.axis_index("lon")
    lat = lax.axis_index("lat")
    lon_x, lon_y = lon // SIDE, lon % SIDE
    east, west = (lon + 1) % NLON, (lon + NLON - 1) % NLON
    south, north = (lat + 1) % NLAT, (lat + NLAT - 1) % NLAT

    def peer(k):
        return ((lon_x + k // SIDE) % SIDE) * SIDE + (lon_y + k % SIDE) % SIDE

    loads = [
        pltpu.make_async_copy(ckpt.at[:, pl.ds(g * CHUNK, CHUNK)], blocks.at[:, pl.ds(g * CHUNK, CHUNK)], in_sem.at[g])
        for g in range(5)
    ]
    loads.append(pltpu.make_async_copy(kmt, levels, in_sem.at[5]))
    loads.append(pltpu.make_async_copy(kappa, kap, in_sem.at[6]))
    for load in loads:
        load.start()

    barrier = pltpu.get_barrier_semaphore()
    for k in range(1, NLON):
        pl.semaphore_signal(barrier, inc=1, device_id={"lon": peer(k), "lat": lat})
    for k in range(1, NLAT):
        pl.semaphore_signal(barrier, inc=1, device_id={"lon": lon, "lat": (lat + k) % NLAT})
    for x in (east, west):
        for y in (north, south):
            pl.semaphore_signal(barrier, inc=1, device_id={"lon": x, "lat": y})

    lane = lax.broadcasted_iota(jnp.int32, (8, 128), 1)
    sub = lax.broadcasted_iota(jnp.int32, (8, 128), 0)
    lane32 = lax.broadcasted_iota(jnp.int32, (32, 128), 1)
    lane160 = lax.broadcasted_iota(jnp.int32, (ROWS, 128), 1)
    sub_w = lax.broadcasted_iota(jnp.int32, (8, 512), 0)

    for g in range(5):
        loads[g].wait()
    flat = parted.reshape(Q * ROWS, 128)
    def spread(g, _):
        for r in range(32):
            q, l = divmod(r * BW, 128)
            a = blocks[:, pl.ds(pl.multiple_of(g * CHUNK + q * 128, 128), 128)]
            if l:
                a = pltpu.roll(a, 128 - l, 1)
            if l + BW > 128:
                b = blocks[:, pl.ds(pl.multiple_of(g * CHUNK + q * 128 + 128, 128), 128)]
                a = jnp.where(lane32 < 128 - l, a, pltpu.roll(b, 128 - l, 1))
            flat[pl.ds(g * 32 + r, 32, stride=ROWS), :] = a
        return 0
    lax.fori_loop(0, 5, spread, 0)

    pl.semaphore_wait(barrier, 26)

    def pack(e):
        one = parted[table[e]]
        two = parted[table[NLON + e]]
        return jnp.where(lane160 < 64, one, pltpu.roll(two, 64, 1))

    def block_copy(k):
        return pltpu.make_async_remote_copy(
            src_ref=packed.at[k], dst_ref=landed.at[lon], send_sem=a2a_s.at[k], recv_sem=a2a_r.at[k],
            device_id={"lon": peer(k), "lat": lat})

    def send(k, _):
        packed[k] = pack(peer(k))
        block_copy(k).start()
        return 0
    lax.fori_loop(1, NLON, send, 0)
    landed[lon] = pack(lon)

    loads[5].wait()
    loads[6].wait()
    for i in range(20):
        rows = pl.ds(i * 8, 8)
        for t in range(4):
            w = min(128, COLS - t * 128)
            at = pl.ds(t * 128, w)
            hk[2, rows, at] = levels[rows, at].astype(f32)
            hk[0, rows, at] = kap[0, rows, at]
            hk[1, rows, at] = kap[1, rows, at]

    def halo_copies(h):
        def copy(n, src, dst, x, y):
            return pltpu.make_async_remote_copy(
                src_ref=src, dst_ref=dst, send_sem=halo_s.at[h, n], recv_sem=halo_r.at[h, n],
                device_id={"lon": x, "lat": y})
        low, high = pl.ds(0, 128), pl.ds(384, 128)
        return [
            copy(0, east_o.at[h], west_i.at[h], east, lat),
            copy(1, west_o.at[h], east_i.at[h], west, lat),
            copy(2, north_o.at[h], south_i.at[h], lon, north),
            copy(3, south_o.at[h], north_i.at[h], lon, south),
            copy(4, north_o.at[h, :, :, low], corner_i.at[h, 0], west, north),
            copy(5, north_o.at[h, :, :, high], corner_i.at[h, 1], east, north),
            copy(6, south_o.at[h, :, :, low], corner_i.at[h, 2], west, south),
            copy(7, south_o.at[h, :, :, high], corner_i.at[h, 3], east, south),
        ]

    def stage_halo(h, ref, last):
        for src, tile, start in ((west_o, 0, 0), (east_o, 3, 92)):
            for group in range(3):
                acc = None
                for ii in range(min(8, 20 - group * 8)):
                    i = group * 8 + ii
                    for f in range(4):
                        v = ref[min(f, last), pl.ds(i * 8, 8), pl.ds(tile * 128, 128)]
                        pos = 16 * ii + 4 * f
                        move = (pos - start) % 128
                        v = pltpu.roll(v, move, 1) if move else v
                        acc = v if acc is None else jnp.where(lane >= pos, v, acc)
                src[h, pl.ds(group * 8, 8), :] = acc
        for i in range(2):
            a, b = min(2 * i, last), min(2 * i + 1, last)
            top, bottom = pl.ds(0, 8), pl.ds(152, 8)
            north_o[h, i] = jnp.where(sub_w < 4, ref[a, top, :], pltpu.roll(ref[b, top, :], 4, 0))
            south_o[h, i] = jnp.where(sub_w < 4, pltpu.roll(ref[a, bottom, :], 4, 0), ref[b, bottom, :])

    def unpack_halo(h, ref, last):
        outer = pl.ds(384, 128)
        for i in range(20):
            rows = pl.ds(i * 8, 8)
            from_e = east_i[h, pl.ds((i // 8) * 8, 8), :]
            from_w = west_i[h, pl.ds((i // 8) * 8, 8), :]
            for f in range(last + 1):
                pos = 16 * (i % 8) + 4 * f
                e = pltpu.roll(from_e, (96 - pos) % 128, 1) if pos != 96 else from_e
                w = pltpu.roll(from_w, (124 - pos) % 128, 1) if pos != 124 else from_w
                own = ref[f, rows, outer]
                ref[f, rows, outer] = jnp.where(lane < 96, own, jnp.where(lane < 112, e, w))
        for f in range(last + 1):
            i, odd = divmod(f, 2)
            s, n = south_i[h, i], north_i[h, i]
            se, sw, ne, nw = (corner_i[h, c, i] for c in range(4))
            if odd:
                s, se, sw = (pltpu.roll(v, 4, 0) for v in (s, se, sw))
            else:
                n, ne, nw = (pltpu.roll(v, 4, 0) for v in (n, ne, nw))
            ref[f, pl.ds(160, 8), :] = jnp.where(sub_w < 4, s, n)
            e = pltpu.roll(jnp.where(sub < 4, se, ne), 96, 1)
            w = pltpu.roll(jnp.where(sub < 4, sw, nw), 32, 1)
            mid = ref[f, pl.ds(160, 8), outer]
            ref[f, pl.ds(160, 8), outer] = jnp.where(lane < 96, mid, jnp.where(lane < 112, e, w))

    stage_halo(0, hk, 2)
    early = halo_copies(0)
    for c in early:
        c.start()
    for c in early:
        c.wait_recv()
    unpack_halo(0, hk, 2)
    inside_s = (lat != NLAT - 1).astype(f32)
    inside_n = (lat != 0).astype(f32)
    edge = hk[2, pl.ds(160, 8), :]
    hk[2, pl.ds(160, 8), :] = jnp.where(sub_w < 4, edge * inside_s, edge * inside_n)

    for k in range(1, NLON):
        block_copy(k).wait_recv()

    def place(n, _):
        f, by = n // BY, n % BY
        level = (f % 2).astype(f32)
        src = [table[2 * NLON + by * BX + bx] for bx in range(BX)]
        second = [jnp.full((8, 128), table[2 * NLON + Q + by * BX + bx], jnp.int32) == 1 for bx in range(BX)]
        for i in range(5):
            rows_in = pl.ds(pl.multiple_of(f * BH + i * 8, 8), 8)
            rows_out = pl.ds(pl.multiple_of(by * BH + i * 8, 8), 8)
            v = []
            for bx in range(BX):
                a = landed[src[bx], rows_in, :]
                o = (BW * bx) % 128
                direct = pltpu.roll(a, o, 1) if o else a
                crossed = pltpu.roll(a, (o + 64) % 128, 1) if (o + 64) % 128 else a
                v.append(jnp.where(second[bx], crossed, direct))
            for t, (x, y, z, p, q) in enumerate(((0, 1, 2, 60, 120), (2, 3, 4, 52, 112), (4, 5, 6, 44, 104), (6, 7, 7, 36, 128))):
                at = pl.ds(t * 128, 128)
                w = jnp.where(lane < p, v[x], jnp.where(lane < q, v[y], v[z]))
                tr[f, rows_out, at] = jnp.where(hk[2, rows_out, at] > level, w, 0.0)
        return 0
    lax.fori_loop(0, 16, place, 0)

    stage_halo(1, tr, 3)
    late = halo_copies(1)
    for c in late:
        c.start()
    for c in late:
        c.wait_recv()
    unpack_halo(1, tr, 3)

    def up(c, p):
        return pltpu.roll(jnp.where(sub_w == 7, p, c), 1, 0)

    def down(c, n):
        return pltpu.roll(jnp.where(sub_w == 0, n, c), 7, 0)

    def to_east(c):
        return pltpu.roll(c, 511, 1)

    def to_west(c):
        return pltpu.roll(c, 1, 1)

    def around(i):
        return rows_of(i), rows_of((i + TILES - 1) % TILES), rows_of((i + 1) % TILES)

    def step(i, store):
        here, prev, after = around(i)
        kc = hk[2, here, :]
        ku, kd, ke = up(kc, hk[2, prev, :]), down(kc, hk[2, after, :]), to_east(kc)
        forcing = None
        depth = None
        for l in range(2):
            wet = (kc > l).astype(f32)
            c = hk[l, here, :]
            ge = jnp.where(jnp.minimum(kc, ke) > l, 0.5 * (c + to_east(c)), 0.0)
            gu = jnp.where(jnp.minimum(kc, ku) > l, 0.5 * (c + up(c, hk[l, prev, :])), 0.0)
            gd = jnp.where(jnp.minimum(kc, kd) > l, 0.5 * (c + down(c, hk[l, after, :])), 0.0)
            new = []
            for t in range(2):
                f = 2 * t + l
                c = tr[f, here, :]
                fe = ge * (to_east(c) - c)
                change = fe - to_west(fe) + gd * (down(c, tr[f, after, :]) - c) + gu * (up(c, tr[f, prev, :]) - c)
                v = wet * (c + change)
                new.append(v)
                if store:
                    for part_t in range(4):
                        w = min(128, COLS - part_t * 128)
                        fresh_t[t, l, here, pl.ds(part_t * 128, w)] = v[:, part_t * 128:part_t * 128 + w]
            temp, salt = new
            dens = wet * (haline * salt - thermal * temp - cabbeling * temp * temp)
            dz = 1.0 + 0.5 * l
            forcing = dens if l == 0 else forcing + dz * dens
            depth = wet if l == 0 else depth + dz * wet
        column = (kc > 0).astype(f32)
        col[here, :] = column
        dep[here, :] = depth
        vs[0, here, :] = column * forcing

    def step_own(i, _):
        step(i, True)
        return 0
    lax.fori_loop(0, TILES - 1, step_own, 0)
    result = pltpu.make_async_copy(fresh_t, out_t, out_sem.at[0])
    result.start()
    step(TILES - 1, False)

    sums = []
    for order in range(3):
        def apply(i, acc, order=order, store=True, add=True):
            here, prev, after = around(i)
            c = vs[order, here, :]
            m = up(c, vs[order, prev, :]) + down(c, vs[order, after, :])
            q = c + 0.5 * m
            v = dep[here, :] * c - col[here, :] * (to_east(q) + to_west(q) + m)
            if store:
                vs[order + 1, here, :] = v
            if add:
                acc = (acc[0] + c * c, acc[1] + c * v)
            return acc
        zero = jnp.zeros((8, 512), f32)
        acc = lax.fori_loop(0, TILES - 1, lambda i, a: apply(i, a, store=order < 2), (zero, zero))
        if order < 2:
            apply(TILES - 1, acc, add=False)
        sums += list(acc)

    tile = jnp.zeros((8, 128), f32)
    for k, s in enumerate(sums):
        s = s[:, :128] + s[:, 128:256] + s[:, 256:384] + jnp.where(lane < 96, s[:, 384:], 0.0)
        tile = jnp.where(sub == k, jnp.sum(s, axis=0, keepdims=True), tile)
    part[0] = tile
    red1[lon] = tile

    def red_copy(n, src, dst, x, y):
        return pltpu.make_async_remote_copy(
            src_ref=src, dst_ref=dst, send_sem=red_s.at[n], recv_sem=red_r.at[n], device_id={"lon": x, "lat": y})

    over_lon = [red_copy(k - 1, part.at[0], red1.at[lon], peer(k), lat) for k in range(1, NLON)]
    for c in over_lon:
        c.start()
    for c in over_lon:
        c.wait_recv()
    tile = red1[0]
    for k in range(1, NLON):
        tile = tile + red1[k]
    part[1] = tile
    red2[lat] = tile
    over_lat = [red_copy(14 + k, part.at[1], red2.at[lat], lon, (lat + k) % NLAT) for k in range(1, NLAT)]
    for c in over_lat:
        c.start()
    for c in over_lat:
        c.wait_recv()
    tile = red2[0]
    for k in range(1, NLAT):
        tile = tile + red2[k]
    tile = jnp.sum(tile, axis=1, keepdims=True)
    nu = [tile[k:k + 1] for k in range(6)]

    def dot(a, b):
        total = None
        for i, x in enumerate(a):
            for j, y in enumerate(b):
                term = x * y * nu[i + j]
                total = term if total is None else total + term
        return total

    def image(a):
        return [SHIFT * a[0]] + [SHIFT * a[k] + a[k - 1] for k in range(1, len(a))] + [a[-1]]

    one = jnp.ones((1, 1), f32)
    x = []
    res, direct, norm = [one], [one], nu[0]
    for k in range(3):
        img = image(direct)
        alpha = norm / dot(direct, img)
        x = [(x[n] + alpha * d) if n < len(x) else alpha * d for n, d in enumerate(direct)]
        if k < 2:
            res = [(res[n] - alpha * d) if n < len(res) else -alpha * d for n, d in enumerate(img)]
            later = dot(res, res)
            beta = later / norm
            direct = [(res[n] + beta * direct[n]) if n < len(direct) else res[n] for n in range(len(res))]
            norm = later

    c0, c1, c2 = (jnp.broadcast_to(v, (8, 128)) for v in x)
    for i in range(20):
        rows = pl.ds(i * 8, 8)
        for t in range(4):
            w = min(128, COLS - t * 128)
            at = pl.ds(t * 128, 128)
            v = c0 * vs[0, rows, at] + c1 * vs[1, rows, at] + c2 * vs[2, rows, at]
            stream[rows, pl.ds(t * 128, w)] = v[:, :w]
    final = pltpu.make_async_copy(stream, out_s, out_sem.at[1])
    final.start()

    for k in range(1, NLON):
        block_copy(k).wait_send()
    for c in early + late + over_lon + over_lat:
        c.wait_send()
    result.wait()
    final.wait()


def body(checkpoint, slot_dest, kmt, kappa):
    table = owners(slot_dest[0], lax.axis_index("lon"))
    sem = pltpu.SemaphoreType.DMA
    vm = pltpu.VMEM
    return pl.pallas_call(
        kernel,
        out_shape=(jax.ShapeDtypeStruct((2, 2, ROWS, COLS), f32), jax.ShapeDtypeStruct((ROWS, COLS), f32)),
        in_specs=[pl.BlockSpec(memory_space=pltpu.SMEM)] + [pl.BlockSpec(memory_space=pl.ANY)] * 3,
        out_specs=[pl.BlockSpec(memory_space=pl.ANY)] * 2,
        scratch_shapes=[
            vm((Q, 9600), f32),
            vm((Q, ROWS, 128), f32),
            vm((NLON, ROWS, 128), f32),
            vm((NLON, ROWS, 128), f32),
            vm((ROWS, COLS), jnp.int32),
            vm((2, ROWS, COLS), f32),
            vm((4, TILES * 8, 512), f32),
            vm((3, TILES * 8, 512), f32),
            vm((2, 24, 128), f32),
            vm((2, 24, 128), f32),
            vm((2, 2, 8, 512), f32),
            vm((2, 2, 8, 512), f32),
            vm((2, 24, 128), f32),
            vm((2, 24, 128), f32),
            vm((2, 2, 8, 512), f32),
            vm((2, 2, 8, 512), f32),
            vm((2, 4, 2, 8, 128), f32),
            vm((3, TILES * 8, 512), f32),
            vm((TILES * 8, 512), f32),
            vm((TILES * 8, 512), f32),
            vm((2, 2, ROWS, COLS), f32),
            vm((ROWS, COLS), f32),
            vm((2, 8, 128), f32),
            vm((NLON, 8, 128), f32),
            vm((NLAT, 8, 128), f32),
            sem((7,)),
            sem((2,)),
            sem((NLON,)),
            sem((NLON,)),
            sem((2, 8)),
            sem((2, 8)),
            sem((22,)),
            sem((22,)),
        ],
        compiler_params=pltpu.CompilerParams(collective_id=0, has_side_effects=True, vmem_limit_bytes=48 << 20),
    )(table, checkpoint[0], kmt, kappa)


def solution(mesh):
    placed = (P("lat", "lon", None), P("lat", None), P("lat", "lon"), P(None, "lat", "lon"))
    return jax.shard_map(
        body,
        mesh=mesh,
        in_specs=placed,
        out_specs=(P(None, None, "lat", "lon"), P("lat", "lon")),
        check_vma=False,
    )
```

```python
import jax
import jax.numpy as jnp
from jax import lax
from jax.experimental import pallas as pl
from jax.experimental.pallas import tpu as pltpu
from jax.sharding import PartitionSpec as P

BW = 60
BH = 40
BX = 8
BY = 4
Q = 32
ROWS = 160
COLS = 480
NLON = 16
NLAT = 8
SIDE = 4
TILES = 21
WIDE = TILES * 8
PART = BH * BW
SHIFT = 6.0
ORDER = (0, 2, 1, 3)
KAPPA, KMT = 4, 6

thermal = 0.25
haline = 0.75
cabbeling = 0.05

f32 = jnp.float32
i32 = jnp.int32


def hops(step):
    return (0, 1, 2, 1)[step]


BAND = [(2, 2), (0, 1), (1, 0), (0, 3), (3, 0), (2, 1), (1, 2), (2, 3), (3, 2), (1, 1), (3, 3), (1, 3), (3, 1), (0, 2), (2, 0)]
EVERY = sorted(
    [(x, y, z, c) for x in range(4) for y in range(4) for z in range(4) for c in range(2) if x or y or z or c],
    key=lambda k: -(hops(k[0]) + hops(k[1]) + hops(k[2])),
)


def kernel(ckpt, dest, kmt, kappa, out_t, out_s,
           blocks, slots, row, table, parted, packed, landed0, landed1, landed2, landed3, levels, kap, al, face,
           strips_o, strips_i, rows_i, corners_i,
           vs, col, dep, fresh_t, stream, part, gathered,
           in_sem, out_sem, a2a_s, a2a_r, halo_s, halo_r, red_s, red_r):
    lon = lax.axis_index("lon")
    lat = lax.axis_index("lat")
    landed = (landed0, landed1, landed2, landed3)
    xs = [lax.rem(lon // SIDE + d, SIDE) * SIDE for d in range(4)]
    ys = [lax.rem(lax.rem(lon, SIDE) + d, SIDE) for d in range(4)]
    zs = [lax.rem(lat // 2 + d, 4) * 2 for d in range(4)]
    cs = [lax.rem(lat + d, 2) for d in range(2)]
    east, west = lax.rem(lon + 1, NLON), lax.rem(lon + NLON - 1, NLON)
    south, north = lax.rem(lat + 1, NLAT), lax.rem(lat + NLAT - 1, NLAT)

    get_slots = pltpu.make_async_copy(dest, slots, in_sem.at[0])
    get_blocks = pltpu.make_async_copy(ckpt, blocks, in_sem.at[1])
    get_kmt = pltpu.make_async_copy(kmt, levels, in_sem.at[2])
    get_kappa = pltpu.make_async_copy(kappa, kap, in_sem.at[3])
    for load in (get_slots, get_blocks, get_kmt, get_kappa):
        load.start()

    barrier = pltpu.get_barrier_semaphore()
    for x, y, z, c in EVERY:
        pl.semaphore_signal(barrier, inc=1, device_id={"lon": xs[x] + ys[y], "lat": zs[z] + cs[c]})

    lane = lax.broadcasted_iota(i32, (8, 128), 1)
    sub = lax.broadcasted_iota(i32, (8, 128), 0)
    lane32 = lax.broadcasted_iota(i32, (32, 128), 1)
    lane40 = lax.broadcasted_iota(i32, (BH, 128), 1)
    sub_w = lax.broadcasted_iota(i32, (8, 512), 0)

    get_slots.wait()
    dst = slots[...]
    owner = dst >> 5
    at = lax.broadcasted_iota(i32, (1, NLON * Q), 1)
    source, slot = at >> 5, at & 31
    count = (owner == lon).astype(i32)
    for d in (1, 2, 4, 8, 16):
        count = count + jnp.where(slot >= d, pltpu.roll(count, d, 1), 0)
    code = 2 * source + jnp.clip(count - 1, 0, 1)
    position = lax.broadcasted_iota(i32, (Q, NLON * Q), 0)
    found = jnp.max(jnp.where(dst == lon * Q + position, code, 0), axis=1, keepdims=True)
    to = jnp.where(source == lon, owner, -1) == lax.broadcasted_iota(i32, (NLON, NLON * Q), 0)
    one = jnp.min(jnp.where(to, slot, Q - 1), axis=1, keepdims=True)
    two = jnp.max(jnp.where(to, slot, 0), axis=1, keepdims=True)
    entries = jnp.concatenate([one, two, found], axis=0)
    diagonal = lax.broadcasted_iota(i32, (64, 128), 0) == lax.broadcasted_iota(i32, (64, 128), 1)
    row[...] = jnp.sum(jnp.where(diagonal, entries, 0), axis=0, keepdims=True)
    to_scalars = pltpu.make_async_copy(row, table, in_sem.at[4])
    to_scalars.start()

    get_blocks.wait()

    def spread(f):
        flat = parted.at[f].reshape(Q * BH, 128)
        for r in range(BH):
            q, l = divmod(f * PART + r * BW, 128)
            a = blocks[:, pl.ds(q * 128, 128)]
            if l:
                a = pltpu.roll(a, 128 - l, 1)
            if l + BW > 128:
                b = blocks[:, pl.ds(q * 128 + 128, 128)]
                a = jnp.where(lane32 < 128 - l, a, pltpu.roll(b, 128 - l, 1))
            flat[pl.ds(r, Q, stride=BH), :] = a

    def pack(f, e):
        a = parted[f, table[0, e]]
        b = parted[f, table[0, NLON + e]]
        return jnp.where(lane40 < 64, a, pltpu.roll(b, 64, 1))

    def send_part(f):
        for k, (x, y) in enumerate(BAND):
            e = xs[x] + ys[y]
            packed[f, k] = pack(f, e)
            pltpu.make_async_remote_copy(
                src_ref=packed.at[f, k], dst_ref=landed[f].at[lon], send_sem=a2a_s.at[f], recv_sem=a2a_r.at[f],
                device_id={"lon": e, "lat": lat}).start()
        landed[f][lon] = pack(f, lon)

    spread(ORDER[0])
    to_scalars.wait()
    pl.semaphore_wait(barrier, len(EVERY))
    for n, f in enumerate(ORDER):
        if n:
            spread(f)
        send_part(f)

    def part_done(sem, f):
        most = landed[f].at[pl.ds(0, NLON - 1)]
        return pltpu.make_async_copy(most, most, sem.at[f])

    def stage_strips(f):
        for side, tile, start in ((0, 3, 92), (1, 0, 0)):
            acc = None
            for i in range(20):
                move = (4 * i - start) % 128
                v = al[f, pl.ds(i * 8, 8), pl.ds(tile * 128, 128)]
                v = pltpu.roll(v, move, 1) if move else v
                acc = v if acc is None else jnp.where(lane >= 4 * i, v, acc)
            strips_o[side, f] = acc

    def start_halo(h, f, n):
        fs = pl.ds(f, n)
        top, bottom, low, high = pl.ds(0, 8), pl.ds(152, 8), pl.ds(0, 128), pl.ds(384, 128)

        def copy(kind, src, dst, x, y):
            pltpu.make_async_remote_copy(
                src_ref=src, dst_ref=dst, send_sem=halo_s.at[h, kind], recv_sem=halo_r.at[h, kind],
                device_id={"lon": x, "lat": y}).start()
        copy(2, al.at[fs, top, low], corners_i.at[0, fs], west, north)
        copy(2, al.at[fs, top, high], corners_i.at[1, fs], east, north)
        copy(2, al.at[fs, bottom, low], corners_i.at[2, fs], west, south)
        copy(2, al.at[fs, bottom, high], corners_i.at[3, fs], east, south)
        copy(0, strips_o.at[0, fs], strips_i.at[0, fs], east, lat)
        copy(0, strips_o.at[1, fs], strips_i.at[1, fs], west, lat)
        copy(1, al.at[fs, top, :], rows_i.at[0, fs], lon, north)
        copy(1, al.at[fs, bottom, :], rows_i.at[1, fs], lon, south)

    def wait_halo(h, f, n):
        fs = pl.ds(f, n)
        for kind, ref in enumerate((strips_i, rows_i, corners_i)):
            for sem in (halo_s, halo_r):
                pltpu.make_async_copy(ref.at[:, fs], ref.at[:, fs], sem.at[h, kind]).wait()

    def unpack_halo(f):
        outer = pl.ds(384, 128)
        from_w, from_e = strips_i[0, f], strips_i[1, f]
        for i in range(20):
            rows = pl.ds(i * 8, 8)
            e = pltpu.roll(from_e, 96 - 4 * i, 1) if i != 24 else from_e
            w = pltpu.roll(from_w, 124 - 4 * i, 1)
            al[f, rows, outer] = jnp.where(lane < 96, al[f, rows, outer], jnp.where(lane < 112, e, w))
        last = jnp.where(sub_w < 4, rows_i[0, f], rows_i[1, f])
        e = pltpu.roll(jnp.where(sub < 4, corners_i[0, f], corners_i[2, f]), 96, 1)
        w = pltpu.roll(jnp.where(sub < 4, corners_i[1, f], corners_i[3, f]), 32, 1)
        al[f, pl.ds(160, 8), pl.ds(0, 384)] = last[:, :384]
        al[f, pl.ds(160, 8), outer] = jnp.where(lane < 96, last[:, 384:], jnp.where(lane < 112, e, w))

    def rows_of(i):
        return pl.ds(pl.multiple_of(i * 8, 8), 8)

    def around(i):
        return rows_of(i), rows_of(lax.rem(i + TILES - 1, TILES)), rows_of(lax.rem(i + 1, TILES))

    def up(c, p):
        return pltpu.roll(jnp.where(sub_w == 7, p, c), 1, 0)

    def down(c, n):
        return pltpu.roll(jnp.where(sub_w == 0, n, c), 7, 0)

    def to_east(c):
        return pltpu.roll(c, 511, 1)

    def to_west(c):
        return pltpu.roll(c, 1, 1)

    get_kmt.wait()
    get_kappa.wait()

    def widen(i, _):
        rows = rows_of(i)
        for t in range(4):
            w = min(128, COLS - t * 128)
            at = pl.ds(t * 128, w)
            al[KMT, rows, at] = levels[rows, at].astype(f32)
            al[KAPPA, rows, at] = kap[0, rows, at]
            al[KAPPA + 1, rows, at] = kap[1, rows, at]
        return 0
    lax.fori_loop(0, 20, widen, 0)
    for f in (4, 5, 6):
        stage_strips(f)
    start_halo(4, 4, 3)
    wait_halo(4, 4, 3)
    for f in (4, 5, 6):
        unpack_halo(f)
    inside_s = (lat != NLAT - 1).astype(f32)
    inside_n = (lat != 0).astype(f32)
    edge = al[KMT, pl.ds(160, 8), :]
    al[KMT, pl.ds(160, 8), :] = jnp.where(sub_w < 4, edge * inside_s, edge * inside_n)

    def faces(i, _):
        here, prev, after = around(i)
        kc = al[KMT, here, :]
        ku, kd, ke = up(kc, al[KMT, prev, :]), down(kc, al[KMT, after, :]), to_east(kc)
        ku, kd, ke = jnp.minimum(kc, ku), jnp.minimum(kc, kd), jnp.minimum(kc, ke)
        for l in range(2):
            c = al[KAPPA + l, here, :]
            face[3 * l, here, :] = jnp.where(ke > l, 0.5 * (c + to_east(c)), 0.0)
            face[3 * l + 1, here, :] = jnp.where(ku > l, 0.5 * (c + up(c, al[KAPPA + l, prev, :])), 0.0)
            face[3 * l + 2, here, :] = jnp.where(kd > l, 0.5 * (c + down(c, al[KAPPA + l, after, :])), 0.0)
        col[here, :] = (kc > 0).astype(f32)
        dep[here, :] = (kc > 0).astype(f32) + 1.5 * (kc > 1).astype(f32)
        return 0
    lax.fori_loop(0, TILES, faces, 0)

    def place(f):
        level = float(f % 2)

        def band(by, _):
            code = [table[0, 32 + by * BX + bx] for bx in range(BX)]
            src = [c >> 1 for c in code]
            second = [jnp.full((8, 128), c & 1, i32) == 1 for c in code]
            for i in range(5):
                rows_out = pl.ds(pl.multiple_of(by * BH + i * 8, 8), 8)
                v = []
                for bx in range(BX):
                    a = landed[f][src[bx], pl.ds(i * 8, 8), :]
                    o = (BW * bx) % 128
                    direct = pltpu.roll(a, o, 1) if o else a
                    crossed = pltpu.roll(a, (o + 64) % 128, 1)
                    v.append(jnp.where(second[bx], crossed, direct))
                for t, (x, y, z, p, q) in enumerate(((0, 1, 2, 60, 120), (2, 3, 4, 52, 112), (4, 5, 6, 44, 104), (6, 7, 7, 36, 128))):
                    at = pl.ds(t * 128, 128)
                    w = jnp.where(lane < p, v[x], jnp.where(lane < q, v[y], v[z]))
                    al[f, rows_out, at] = jnp.where(al[KMT, rows_out, at] > level, w, 0.0)
            return 0
        lax.fori_loop(0, BY, band, 0)

    def diffuse(f, first):
        t, l = divmod(f, 2)
        dz = 1.0 + 0.5 * l

        def tile(i, store):
            here, prev, after = around(i)
            c = al[f, here, :]
            fe = face[3 * l, here, :] * (to_east(c) - c)
            change = fe - to_west(fe)
            change = change + face[3 * l + 1, here, :] * (up(c, al[f, prev, :]) - c)
            change = change + face[3 * l + 2, here, :] * (down(c, al[f, after, :]) - c)
            v = jnp.where(al[KMT, here, :] > float(l), c + change, 0.0)
            if store:
                for p in range(4):
                    w = min(128, COLS - p * 128)
                    fresh_t[t, l, here, pl.ds(p * 128, w)] = v[:, p * 128:p * 128 + w]
            share = (dz * haline) * v if t else (-dz) * (thermal * v + cabbeling * v * v)
            vs[0, here, :] = share if first else vs[0, here, :] + share

        def several(j, _):
            for d in range(2):
                tile(2 * j + d, True)
            return 0
        lax.fori_loop(0, 10, several, 0)
        tile(TILES - 1, False)

    for n, f in enumerate(ORDER):
        part_done(a2a_r, f).wait()
        place(f)
        stage_strips(f)
        start_halo(f, f, 1)
        if n:
            g = ORDER[n - 1]
            wait_halo(g, g, 1)
            unpack_halo(g)
            diffuse(g, n == 1)
    g = ORDER[3]
    wait_halo(g, g, 1)
    unpack_halo(g)
    diffuse(g, False)
    result = pltpu.make_async_copy(fresh_t, out_t, out_sem.at[0])
    result.start()

    sums = []
    for order in range(3):
        def apply(i, acc, order=order, add=True):
            here, prev, after = around(i)
            c = vs[order, here, :]
            m = up(c, vs[order, prev, :]) + down(c, vs[order, after, :])
            q = c + 0.5 * m
            v = dep[here, :] * c - col[here, :] * (to_east(q) + to_west(q) + m)
            if order < 2:
                vs[order + 1, here, :] = v
            return (acc[0] + c * c, acc[1] + c * v) if add else acc

        def several(j, acc, apply=apply):
            for d in range(4):
                acc = apply(4 * j + d, acc)
            return acc
        zero = jnp.zeros((8, 512), f32)
        acc = lax.fori_loop(0, 5, several, (zero, zero))
        if order < 2:
            apply(TILES - 1, acc, add=False)
        sums += list(acc)

    tile = jnp.zeros((8, 128), f32)
    for k, s in enumerate(sums):
        s = s[:, :128] + s[:, 128:256] + s[:, 256:384] + jnp.where(lane < 96, s[:, 384:], 0.0)
        tile = jnp.where(sub == k, jnp.sum(s, axis=0, keepdims=True), tile)
    tile = jnp.where(sub == lane, jnp.sum(tile, axis=1, keepdims=True), 0.0)
    mine = jnp.sum(tile, axis=0, keepdims=True)
    part[...] = mine
    for k, (x, y, z, c) in enumerate(EVERY):
        pltpu.make_async_remote_copy(
            src_ref=part, dst_ref=gathered.at[k], send_sem=red_s, recv_sem=red_r,
            device_id={"lon": xs[x] + ys[y], "lat": zs[z] + cs[c]}).start()
    pltpu.make_async_copy(gathered, gathered, red_r).wait()
    total = mine + jnp.sum(gathered[...], axis=0)
    nu = [total[:, k:k + 1] for k in range(6)]

    def dot(a, b):
        total = None
        for i, x in enumerate(a):
            for j, y in enumerate(b):
                term = x * y * nu[i + j]
                total = term if total is None else total + term
        return total

    def image(a):
        return [SHIFT * a[0]] + [SHIFT * a[k] + a[k - 1] for k in range(1, len(a))] + [a[-1]]

    unit = jnp.ones((1, 1), f32)
    x = []
    res, direct, norm = [unit], [unit], nu[0]
    for k in range(3):
        img = image(direct)
        alpha = norm / dot(direct, img)
        x = [(x[n] + alpha * d) if n < len(x) else alpha * d for n, d in enumerate(direct)]
        if k < 2:
            res = [(res[n] - alpha * d) if n < len(res) else -alpha * d for n, d in enumerate(img)]
            later = dot(res, res)
            beta = later / norm
            direct = [(res[n] + beta * direct[n]) if n < len(direct) else res[n] for n in range(len(res))]
            norm = later

    c0, c1, c2 = (jnp.broadcast_to(v, (8, 128)) for v in x)
    for i in range(20):
        rows = pl.ds(i * 8, 8)
        for t in range(4):
            w = min(128, COLS - t * 128)
            at = pl.ds(t * 128, 128)
            v = c0 * vs[0, rows, at] + c1 * vs[1, rows, at] + c2 * vs[2, rows, at]
            stream[rows, pl.ds(t * 128, w)] = v[:, :w]
    final = pltpu.make_async_copy(stream, out_s, out_sem.at[1])
    final.start()

    for f in ORDER:
        part_done(a2a_s, f).wait()
    pltpu.make_async_copy(gathered, gathered, red_s).wait()
    result.wait()
    final.wait()


def body(checkpoint, slot_dest, kmt, kappa):
    sem = pltpu.SemaphoreType.DMA
    vm = pltpu.VMEM
    return pl.pallas_call(
        kernel,
        out_shape=(jax.ShapeDtypeStruct((2, 2, ROWS, COLS), f32), jax.ShapeDtypeStruct((ROWS, COLS), f32)),
        in_specs=[pl.BlockSpec(memory_space=pl.ANY)] * 4,
        out_specs=[pl.BlockSpec(memory_space=pl.ANY)] * 2,
        scratch_shapes=[
            vm((Q, 9600), f32),
            vm((1, NLON * Q), i32),
            vm((1, 128), i32),
            pltpu.SMEM((1, 128), i32),
            vm((4, Q, BH, 128), f32),
            vm((4, NLON - 1, BH, 128), f32),
            *[vm((NLON, BH, 128), f32)] * 4,
            vm((ROWS, COLS), i32),
            vm((2, ROWS, COLS), f32),
            vm((7, WIDE, 512), f32),
            vm((6, WIDE, 512), f32),
            vm((2, 7, 8, 128), f32),
            vm((2, 7, 8, 128), f32),
            vm((2, 7, 8, 512), f32),
            vm((4, 7, 8, 128), f32),
            vm((3, WIDE, 512), f32),
            vm((WIDE, 512), f32),
            vm((WIDE, 512), f32),
            vm((2, 2, ROWS, COLS), f32),
            vm((ROWS, COLS), f32),
            vm((1, 128), f32),
            vm((NLON * NLAT - 1, 1, 128), f32),
            sem((5,)),
            sem((2,)),
            sem((4,)),
            sem((4,)),
            sem((5, 3)),
            sem((5, 3)),
            sem,
            sem,
        ],
        compiler_params=pltpu.CompilerParams(collective_id=0, has_side_effects=True, vmem_limit_bytes=60 << 20),
    )(checkpoint[0], slot_dest, kmt, kappa)


def solution(mesh):
    placed = (P("lat", "lon", None), P("lat", None), P("lat", "lon"), P(None, "lat", "lon"))
    return jax.shard_map(
        body,
        mesh=mesh,
        in_specs=placed,
        out_specs=(P(None, None, "lat", "lon"), P("lat", "lon")),
        check_vma=False,
    )
```

```python
import jax
import jax.numpy as jnp
from jax import lax
from jax.experimental import pallas as pl
from jax.experimental.pallas import tpu as pltpu
from jax.sharding import PartitionSpec as P

BW = 60
BH = 40
BX = 8
BY = 4
Q = 32
ROWS = 160
COLS = 480
NLON = 16
NLAT = 8
SIDE = 4
TILES = 21
WIDE = TILES * 8
PART = BH * BW
SHIFT = 6.0
ORDER = (0, 2, 1, 3)
KAPPA, KMT = 4, 6

thermal = 0.25
haline = 0.75
cabbeling = 0.05

f32 = jnp.float32
i32 = jnp.int32


def hops(step):
    return (0, 1, 2, 1)[step]


BAND = [(2, 2), (0, 1), (1, 0), (0, 3), (3, 0), (2, 1), (1, 2), (2, 3), (3, 2), (1, 1), (3, 3), (1, 3), (3, 1), (0, 2), (2, 0)]
EVERY = sorted(
    [(x, y, z, c) for x in range(4) for y in range(4) for z in range(4) for c in range(2) if x or y or z or c],
    key=lambda k: -(hops(k[0]) + hops(k[1]) + hops(k[2])),
)


def kernel(ckpt, dest, kmt, kappa, out_t, out_s,
           blocks, slots, row, table, parted, packed, landed0, landed1, landed2, landed3, levels, kap, al, face,
           strips_o, strips_i, rows_i, corners_i,
           vs, col, dep, fresh_t, stream, part, gathered,
           in_sem, out_sem, a2a_s, a2a_r, halo_s, halo_r, red_s, red_r):
    lon = lax.axis_index("lon")
    lat = lax.axis_index("lat")
    landed = (landed0, landed1, landed2, landed3)
    xs = [lax.rem(lon // SIDE + d, SIDE) * SIDE for d in range(4)]
    ys = [lax.rem(lax.rem(lon, SIDE) + d, SIDE) for d in range(4)]
    zs = [lax.rem(lat // 2 + d, 4) * 2 for d in range(4)]
    cs = [lax.rem(lat + d, 2) for d in range(2)]
    east, west = lax.rem(lon + 1, NLON), lax.rem(lon + NLON - 1, NLON)
    south, north = lax.rem(lat + 1, NLAT), lax.rem(lat + NLAT - 1, NLAT)

    get_slots = pltpu.make_async_copy(dest, slots, in_sem.at[0])
    get_blocks = pltpu.make_async_copy(ckpt, blocks, in_sem.at[1])
    get_kmt = pltpu.make_async_copy(kmt, levels, in_sem.at[2])
    get_kappa = pltpu.make_async_copy(kappa, kap, in_sem.at[3])
    for load in (get_slots, get_blocks, get_kmt, get_kappa):
        load.start()

    barrier = pltpu.get_barrier_semaphore()
    for x, y, z, c in EVERY:
        pl.semaphore_signal(barrier, inc=1, device_id={"lon": xs[x] + ys[y], "lat": zs[z] + cs[c]})

    lane = lax.broadcasted_iota(i32, (8, 128), 1)
    sub = lax.broadcasted_iota(i32, (8, 128), 0)
    lane32 = lax.broadcasted_iota(i32, (32, 128), 1)
    lane40 = lax.broadcasted_iota(i32, (BH, 128), 1)
    sub_w = lax.broadcasted_iota(i32, (8, 512), 0)

    get_slots.wait()
    dst = slots[...]
    owner = dst >> 5
    at = lax.broadcasted_iota(i32, (1, NLON * Q), 1)
    source, slot = at >> 5, at & 31
    count = (owner == lon).astype(i32)
    for d in (1, 2, 4, 8, 16):
        count = count + jnp.where(slot >= d, pltpu.roll(count, d, 1), 0)
    code = 2 * source + jnp.clip(count - 1, 0, 1)
    position = lax.broadcasted_iota(i32, (Q, NLON * Q), 0)
    found = jnp.max(jnp.where(dst == lon * Q + position, code, 0), axis=1, keepdims=True)
    to = jnp.where(source == lon, owner, -1) == lax.broadcasted_iota(i32, (NLON, NLON * Q), 0)
    one = jnp.min(jnp.where(to, slot, Q - 1), axis=1, keepdims=True)
    two = jnp.max(jnp.where(to, slot, 0), axis=1, keepdims=True)
    entries = jnp.concatenate([one, two, found], axis=0)
    diagonal = lax.broadcasted_iota(i32, (64, 128), 0) == lax.broadcasted_iota(i32, (64, 128), 1)
    row[...] = jnp.sum(jnp.where(diagonal, entries, 0), axis=0, keepdims=True)
    to_scalars = pltpu.make_async_copy(row, table, in_sem.at[4])
    to_scalars.start()

    get_blocks.wait()

    def spread(f):
        flat = parted.at[f].reshape(Q * BH, 128)
        for r in range(BH):
            q, l = divmod(f * PART + r * BW, 128)
            a = blocks[:, pl.ds(q * 128, 128)]
            if l:
                a = pltpu.roll(a, 128 - l, 1)
            if l + BW > 128:
                b = blocks[:, pl.ds(q * 128 + 128, 128)]
                a = jnp.where(lane32 < 128 - l, a, pltpu.roll(b, 128 - l, 1))
            flat[pl.ds(r, Q, stride=BH), :] = a

    def pack(f, e):
        a = parted[f, table[0, e]]
        b = parted[f, table[0, NLON + e]]
        return jnp.where(lane40 < 64, a, pltpu.roll(b, 64, 1))

    def send_part(f):
        for k, (x, y) in enumerate(BAND):
            e = xs[x] + ys[y]
            packed[f, k] = pack(f, e)
            pltpu.make_async_remote_copy(
                src_ref=packed.at[f, k], dst_ref=landed[f].at[lon], send_sem=a2a_s.at[f], recv_sem=a2a_r.at[f],
                device_id={"lon": e, "lat": lat}).start()
        landed[f][lon] = pack(f, lon)

    def part_done(sem, f):
        most = landed[f].at[pl.ds(0, NLON - 1)]
        return pltpu.make_async_copy(most, most, sem.at[f])

    def stage_strips(f):
        for side, tile, start in ((0, 3, 92), (1, 0, 0)):
            acc = None
            for i in range(20):
                move = (4 * i - start) % 128
                v = al[f, pl.ds(i * 8, 8), pl.ds(tile * 128, 128)]
                v = pltpu.roll(v, move, 1) if move else v
                acc = v if acc is None else jnp.where(lane >= 4 * i, v, acc)
            strips_o[side, f] = acc

    def start_halo(h, f, n):
        fs = pl.ds(f, n)
        top, bottom, low, high = pl.ds(0, 8), pl.ds(152, 8), pl.ds(0, 128), pl.ds(384, 128)

        def copy(kind, src, dst, x, y):
            pltpu.make_async_remote_copy(
                src_ref=src, dst_ref=dst, send_sem=halo_s.at[h, kind], recv_sem=halo_r.at[h, kind],
                device_id={"lon": x, "lat": y}).start()
        copy(2, al.at[fs, top, low], corners_i.at[0, fs], west, north)
        copy(2, al.at[fs, top, high], corners_i.at[1, fs], east, north)
        copy(2, al.at[fs, bottom, low], corners_i.at[2, fs], west, south)
        copy(2, al.at[fs, bottom, high], corners_i.at[3, fs], east, south)
        copy(0, strips_o.at[0, fs], strips_i.at[0, fs], east, lat)
        copy(0, strips_o.at[1, fs], strips_i.at[1, fs], west, lat)
        copy(1, al.at[fs, top, :], rows_i.at[0, fs], lon, north)
        copy(1, al.at[fs, bottom, :], rows_i.at[1, fs], lon, south)

    def wait_halo(h, f, n):
        fs = pl.ds(f, n)
        for kind, ref in enumerate((strips_i, rows_i, corners_i)):
            for sem in (halo_s, halo_r):
                pltpu.make_async_copy(ref.at[:, fs], ref.at[:, fs], sem.at[h, kind]).wait()

    def unpack_halo(f):
        outer = pl.ds(384, 128)
        from_w, from_e = strips_i[0, f], strips_i[1, f]
        for i in range(20):
            rows = pl.ds(i * 8, 8)
            e = pltpu.roll(from_e, 96 - 4 * i, 1) if i != 24 else from_e
            w = pltpu.roll(from_w, 124 - 4 * i, 1)
            al[f, rows, outer] = jnp.where(lane < 96, al[f, rows, outer], jnp.where(lane < 112, e, w))
        last = jnp.where(sub_w < 4, rows_i[0, f], rows_i[1, f])
        e = pltpu.roll(jnp.where(sub < 4, corners_i[0, f], corners_i[2, f]), 96, 1)
        w = pltpu.roll(jnp.where(sub < 4, corners_i[1, f], corners_i[3, f]), 32, 1)
        al[f, pl.ds(160, 8), pl.ds(0, 384)] = last[:, :384]
        al[f, pl.ds(160, 8), outer] = jnp.where(lane < 96, last[:, 384:], jnp.where(lane < 112, e, w))

    def rows_of(i):
        return pl.ds(pl.multiple_of(i * 8, 8), 8)

    def around(i):
        return rows_of(i), rows_of(lax.rem(i + TILES - 1, TILES)), rows_of(lax.rem(i + 1, TILES))

    def up(c, p):
        return pltpu.roll(jnp.where(sub_w == 7, p, c), 1, 0)

    def down(c, n):
        return pltpu.roll(jnp.where(sub_w == 0, n, c), 7, 0)

    def to_east(c):
        return pltpu.roll(c, 511, 1)

    def to_west(c):
        return pltpu.roll(c, 1, 1)

    get_kmt.wait()
    get_kappa.wait()

    def widen(i, _):
        rows = rows_of(i)
        for t in range(4):
            w = min(128, COLS - t * 128)
            at = pl.ds(t * 128, w)
            al[KMT, rows, at] = levels[rows, at].astype(f32)
            al[KAPPA, rows, at] = kap[0, rows, at]
            al[KAPPA + 1, rows, at] = kap[1, rows, at]
        return 0
    lax.fori_loop(0, 20, widen, 0)
    for f in (4, 5, 6):
        stage_strips(f)
    spread(ORDER[0])
    to_scalars.wait()
    pl.semaphore_wait(barrier, len(EVERY))
    start_halo(4, 4, 3)
    send_part(ORDER[0])
    for f in ORDER[1:]:
        spread(f)
        if f == ORDER[1]:
            send_part(f)

    wait_halo(4, 4, 3)
    for f in (4, 5, 6):
        unpack_halo(f)
    inside_s = (lat != NLAT - 1).astype(f32)
    inside_n = (lat != 0).astype(f32)
    edge = al[KMT, pl.ds(160, 8), :]
    al[KMT, pl.ds(160, 8), :] = jnp.where(sub_w < 4, edge * inside_s, edge * inside_n)

    def faces(i, _):
        here, prev, after = around(i)
        kc = al[KMT, here, :]
        ku, kd, ke = up(kc, al[KMT, prev, :]), down(kc, al[KMT, after, :]), to_east(kc)
        ku, kd, ke = jnp.minimum(kc, ku), jnp.minimum(kc, kd), jnp.minimum(kc, ke)
        for l in range(2):
            c = al[KAPPA + l, here, :]
            face[3 * l, here, :] = jnp.where(ke > l, 0.5 * (c + to_east(c)), 0.0)
            face[3 * l + 1, here, :] = jnp.where(ku > l, 0.5 * (c + up(c, al[KAPPA + l, prev, :])), 0.0)
            face[3 * l + 2, here, :] = jnp.where(kd > l, 0.5 * (c + down(c, al[KAPPA + l, after, :])), 0.0)
        col[here, :] = (kc > 0).astype(f32)
        dep[here, :] = (kc > 0).astype(f32) + 1.5 * (kc > 1).astype(f32)
        return 0
    lax.fori_loop(0, TILES, faces, 0)

    def place(f):
        level = float(f % 2)

        def band(by, _):
            code = [table[0, 32 + by * BX + bx] for bx in range(BX)]
            src = [c >> 1 for c in code]
            second = [jnp.full((8, 128), c & 1, i32) == 1 for c in code]
            for i in range(5):
                rows_out = pl.ds(pl.multiple_of(by * BH + i * 8, 8), 8)
                v = []
                for bx in range(BX):
                    a = landed[f][src[bx], pl.ds(i * 8, 8), :]
                    o = (BW * bx) % 128
                    direct = pltpu.roll(a, o, 1) if o else a
                    crossed = pltpu.roll(a, (o + 64) % 128, 1)
                    v.append(jnp.where(second[bx], crossed, direct))
                for t, (x, y, z, p, q) in enumerate(((0, 1, 2, 60, 120), (2, 3, 4, 52, 112), (4, 5, 6, 44, 104), (6, 7, 7, 36, 128))):
                    at = pl.ds(t * 128, 128)
                    w = jnp.where(lane < p, v[x], jnp.where(lane < q, v[y], v[z]))
                    al[f, rows_out, at] = jnp.where(al[KMT, rows_out, at] > level, w, 0.0)
            return 0
        lax.fori_loop(0, BY, band, 0)

    def diffuse(f, first):
        t, l = divmod(f, 2)
        dz = 1.0 + 0.5 * l

        def tile(i, store):
            here, prev, after = around(i)
            c = al[f, here, :]
            fe = face[3 * l, here, :] * (to_east(c) - c)
            change = fe - to_west(fe)
            change = change + face[3 * l + 1, here, :] * (up(c, al[f, prev, :]) - c)
            change = change + face[3 * l + 2, here, :] * (down(c, al[f, after, :]) - c)
            v = jnp.where(al[KMT, here, :] > float(l), c + change, 0.0)
            if store:
                for p in range(4):
                    w = min(128, COLS - p * 128)
                    fresh_t[t, l, here, pl.ds(p * 128, w)] = v[:, p * 128:p * 128 + w]
            share = (dz * haline) * v if t else (-dz) * (thermal * v + cabbeling * v * v)
            vs[0, here, :] = share if first else vs[0, here, :] + share

        def several(j, _):
            for d in range(2):
                tile(2 * j + d, True)
            return 0
        lax.fori_loop(0, 10, several, 0)
        tile(TILES - 1, False)

    for n, f in enumerate(ORDER):
        part_done(a2a_r, f).wait()
        place(f)
        stage_strips(f)
        start_halo(f, f, 1)
        if n < 2:
            send_part(ORDER[n + 2])
        if n:
            g = ORDER[n - 1]
            wait_halo(g, g, 1)
            unpack_halo(g)
            diffuse(g, n == 1)
    g = ORDER[3]
    wait_halo(g, g, 1)
    unpack_halo(g)
    diffuse(g, False)
    result = pltpu.make_async_copy(fresh_t, out_t, out_sem.at[0])
    result.start()

    sums = []
    for order in range(3):
        def apply(i, acc, order=order, add=True):
            here, prev, after = around(i)
            c = vs[order, here, :]
            m = up(c, vs[order, prev, :]) + down(c, vs[order, after, :])
            q = c + 0.5 * m
            v = dep[here, :] * c - col[here, :] * (to_east(q) + to_west(q) + m)
            if order < 2:
                vs[order + 1, here, :] = v
            return (acc[0] + c * c, acc[1] + c * v) if add else acc

        def several(j, acc, apply=apply):
            for d in range(4):
                acc = apply(4 * j + d, acc)
            return acc
        zero = jnp.zeros((8, 512), f32)
        acc = lax.fori_loop(0, 5, several, (zero, zero))
        if order < 2:
            apply(TILES - 1, acc, add=False)
        sums += list(acc)

    tile = jnp.zeros((8, 128), f32)
    for k, s in enumerate(sums):
        s = s[:, :128] + s[:, 128:256] + s[:, 256:384] + jnp.where(lane < 96, s[:, 384:], 0.0)
        tile = jnp.where(sub == k, jnp.sum(s, axis=0, keepdims=True), tile)
    tile = jnp.where(sub == lane, jnp.sum(tile, axis=1, keepdims=True), 0.0)
    mine = jnp.sum(tile, axis=0, keepdims=True)
    part[...] = mine
    for k, (x, y, z, c) in enumerate(EVERY):
        pltpu.make_async_remote_copy(
            src_ref=part, dst_ref=gathered.at[k], send_sem=red_s, recv_sem=red_r,
            device_id={"lon": xs[x] + ys[y], "lat": zs[z] + cs[c]}).start()
    pltpu.make_async_copy(gathered, gathered, red_r).wait()
    total = mine + jnp.sum(gathered[...], axis=0)
    nu = [total[:, k:k + 1] for k in range(6)]

    def dot(a, b):
        total = None
        for i, x in enumerate(a):
            for j, y in enumerate(b):
                term = x * y * nu[i + j]
                total = term if total is None else total + term
        return total

    def image(a):
        return [SHIFT * a[0]] + [SHIFT * a[k] + a[k - 1] for k in range(1, len(a))] + [a[-1]]

    unit = jnp.ones((1, 1), f32)
    x = []
    res, direct, norm = [unit], [unit], nu[0]
    for k in range(3):
        img = image(direct)
        alpha = norm / dot(direct, img)
        x = [(x[n] + alpha * d) if n < len(x) else alpha * d for n, d in enumerate(direct)]
        if k < 2:
            res = [(res[n] - alpha * d) if n < len(res) else -alpha * d for n, d in enumerate(img)]
            later = dot(res, res)
            beta = later / norm
            direct = [(res[n] + beta * direct[n]) if n < len(direct) else res[n] for n in range(len(res))]
            norm = later

    c0, c1, c2 = (jnp.broadcast_to(v, (8, 128)) for v in x)
    for i in range(20):
        rows = pl.ds(i * 8, 8)
        for t in range(4):
            w = min(128, COLS - t * 128)
            at = pl.ds(t * 128, 128)
            v = c0 * vs[0, rows, at] + c1 * vs[1, rows, at] + c2 * vs[2, rows, at]
            stream[rows, pl.ds(t * 128, w)] = v[:, :w]
    final = pltpu.make_async_copy(stream, out_s, out_sem.at[1])
    final.start()

    for f in ORDER:
        part_done(a2a_s, f).wait()
    pltpu.make_async_copy(gathered, gathered, red_s).wait()
    result.wait()
    final.wait()


def body(checkpoint, slot_dest, kmt, kappa):
    sem = pltpu.SemaphoreType.DMA
    vm = pltpu.VMEM
    return pl.pallas_call(
        kernel,
        out_shape=(jax.ShapeDtypeStruct((2, 2, ROWS, COLS), f32), jax.ShapeDtypeStruct((ROWS, COLS), f32)),
        in_specs=[pl.BlockSpec(memory_space=pl.ANY)] * 4,
        out_specs=[pl.BlockSpec(memory_space=pl.ANY)] * 2,
        scratch_shapes=[
            vm((Q, 9600), f32),
            vm((1, NLON * Q), i32),
            vm((1, 128), i32),
            pltpu.SMEM((1, 128), i32),
            vm((4, Q, BH, 128), f32),
            vm((4, NLON - 1, BH, 128), f32),
            *[vm((NLON, BH, 128), f32)] * 4,
            vm((ROWS, COLS), i32),
            vm((2, ROWS, COLS), f32),
            vm((7, WIDE, 512), f32),
            vm((6, WIDE, 512), f32),
            vm((2, 7, 8, 128), f32),
            vm((2, 7, 8, 128), f32),
            vm((2, 7, 8, 512), f32),
            vm((4, 7, 8, 128), f32),
            vm((3, WIDE, 512), f32),
            vm((WIDE, 512), f32),
            vm((WIDE, 512), f32),
            vm((2, 2, ROWS, COLS), f32),
            vm((ROWS, COLS), f32),
            vm((1, 128), f32),
            vm((NLON * NLAT - 1, 1, 128), f32),
            sem((5,)),
            sem((2,)),
            sem((4,)),
            sem((4,)),
            sem((5, 3)),
            sem((5, 3)),
            sem,
            sem,
        ],
        compiler_params=pltpu.CompilerParams(collective_id=0, has_side_effects=True, vmem_limit_bytes=60 << 20),
    )(checkpoint[0], slot_dest, kmt, kappa)


def solution(mesh):
    placed = (P("lat", "lon", None), P("lat", None), P("lat", "lon"), P(None, "lat", "lon"))
    return jax.shard_map(
        body,
        mesh=mesh,
        in_specs=placed,
        out_specs=(P(None, None, "lat", "lon"), P("lat", "lon")),
        check_vma=False,
    )
```

```python
import jax
import jax.numpy as jnp
from jax import lax
from jax.experimental import pallas as pl
from jax.experimental.pallas import tpu as pltpu
from jax.sharding import PartitionSpec as P

BW = 60
BH = 40
BX = 8
BY = 4
Q = 32
ROWS = 160
COLS = 480
NLON = 16
NLAT = 8
SIDE = 4
TILES = 21
WIDE = TILES * 8
PART = BH * BW
SHIFT = 6.0
ORDER = (0, 2, 1, 3)
KAPPA, KMT = 4, 6

thermal = 0.25
haline = 0.75
cabbeling = 0.05

f32 = jnp.float32
i32 = jnp.int32


def hops(step):
    return (0, 1, 2, 1)[step]


BAND = [(2, 2), (0, 1), (1, 0), (0, 3), (3, 0), (2, 1), (1, 2), (2, 3), (3, 2), (1, 1), (3, 3), (1, 3), (3, 1), (0, 2), (2, 0)]
EVERY = sorted(
    [(x, y, z, c) for x in range(4) for y in range(4) for z in range(4) for c in range(2) if x or y or z or c],
    key=lambda k: -(hops(k[0]) + hops(k[1]) + hops(k[2])),
)


def kernel(ckpt, dest, kmt, kappa, out_t, out_v, out_n,
           blocks, slots, row, table, parted, packed, landed0, landed1, landed2, landed3, levels, kap, al, face,
           strips_o, strips_i, rows_i, corners_i,
           vs, col, dep, fresh_t, part, summed, gathered,
           in_sem, out_sem, a2a_s, a2a_r, halo_s, halo_r, red_s, red_r):
    lon = lax.axis_index("lon")
    lat = lax.axis_index("lat")
    landed = (landed0, landed1, landed2, landed3)
    xs = [lax.rem(lon // SIDE + d, SIDE) * SIDE for d in range(4)]
    ys = [lax.rem(lax.rem(lon, SIDE) + d, SIDE) for d in range(4)]
    zs = [lax.rem(lat // 2 + d, 4) * 2 for d in range(4)]
    cs = [lax.rem(lat + d, 2) for d in range(2)]
    east, west = lax.rem(lon + 1, NLON), lax.rem(lon + NLON - 1, NLON)
    south, north = lax.rem(lat + 1, NLAT), lax.rem(lat + NLAT - 1, NLAT)

    get_slots = pltpu.make_async_copy(dest, slots, in_sem.at[0])
    get_blocks = pltpu.make_async_copy(ckpt, blocks, in_sem.at[1])
    get_kmt = pltpu.make_async_copy(kmt, levels, in_sem.at[2])
    get_kappa = pltpu.make_async_copy(kappa, kap, in_sem.at[3])
    for load in (get_slots, get_blocks, get_kmt, get_kappa):
        load.start()

    barrier = pltpu.get_barrier_semaphore()
    for x, y, z, c in EVERY:
        pl.semaphore_signal(barrier, inc=1, device_id={"lon": xs[x] + ys[y], "lat": zs[z] + cs[c]})

    lane = lax.broadcasted_iota(i32, (8, 128), 1)
    sub = lax.broadcasted_iota(i32, (8, 128), 0)
    lane32 = lax.broadcasted_iota(i32, (32, 128), 1)
    lane40 = lax.broadcasted_iota(i32, (BH, 128), 1)
    sub_w = lax.broadcasted_iota(i32, (8, 512), 0)

    get_slots.wait()
    dst = slots[...]
    owner = dst >> 5
    at = lax.broadcasted_iota(i32, (1, NLON * Q), 1)
    source, slot = at >> 5, at & 31
    count = (owner == lon).astype(i32)
    for d in (1, 2, 4, 8, 16):
        count = count + jnp.where(slot >= d, pltpu.roll(count, d, 1), 0)
    code = 2 * source + jnp.clip(count - 1, 0, 1)
    position = lax.broadcasted_iota(i32, (Q, NLON * Q), 0)
    found = jnp.max(jnp.where(dst == lon * Q + position, code, 0), axis=1, keepdims=True)
    to = jnp.where(source == lon, owner, -1) == lax.broadcasted_iota(i32, (NLON, NLON * Q), 0)
    one = jnp.min(jnp.where(to, slot, Q - 1), axis=1, keepdims=True)
    two = jnp.max(jnp.where(to, slot, 0), axis=1, keepdims=True)
    entries = jnp.concatenate([one, two, found], axis=0)
    diagonal = lax.broadcasted_iota(i32, (64, 128), 0) == lax.broadcasted_iota(i32, (64, 128), 1)
    row[...] = jnp.sum(jnp.where(diagonal, entries, 0), axis=0, keepdims=True)
    to_scalars = pltpu.make_async_copy(row, table, in_sem.at[4])
    to_scalars.start()

    get_blocks.wait()

    def spread(f):
        flat = parted.at[f].reshape(Q * BH, 128)
        for r in range(BH):
            q, l = divmod(f * PART + r * BW, 128)
            a = blocks[:, pl.ds(q * 128, 128)]
            if l:
                a = pltpu.roll(a, 128 - l, 1)
            if l + BW > 128:
                b = blocks[:, pl.ds(q * 128 + 128, 128)]
                a = jnp.where(lane32 < 128 - l, a, pltpu.roll(b, 128 - l, 1))
            flat[pl.ds(r, Q, stride=BH), :] = a

    def pack(f, e):
        a = parted[f, table[0, e]]
        b = parted[f, table[0, NLON + e]]
        return jnp.where(lane40 < 64, a, pltpu.roll(b, 64, 1))

    def send_part(f):
        for k, (x, y) in enumerate(BAND):
            e = xs[x] + ys[y]
            packed[f, k] = pack(f, e)
            pltpu.make_async_remote_copy(
                src_ref=packed.at[f, k], dst_ref=landed[f].at[lon], send_sem=a2a_s.at[f], recv_sem=a2a_r.at[f],
                device_id={"lon": e, "lat": lat}).start()
        landed[f][lon] = pack(f, lon)

    def part_done(sem, f):
        most = landed[f].at[pl.ds(0, NLON - 1)]
        return pltpu.make_async_copy(most, most, sem.at[f])

    def stage_strips(f):
        for side, tile, start in ((0, 3, 92), (1, 0, 0)):
            acc = None
            for i in range(20):
                move = (4 * i - start) % 128
                v = al[f, pl.ds(i * 8, 8), pl.ds(tile * 128, 128)]
                v = pltpu.roll(v, move, 1) if move else v
                acc = v if acc is None else jnp.where(lane >= 4 * i, v, acc)
            strips_o[side, f] = acc

    def start_halo(h, f, n):
        fs = pl.ds(f, n)
        top, bottom, low, high = pl.ds(0, 8), pl.ds(152, 8), pl.ds(0, 128), pl.ds(384, 128)

        def copy(kind, src, dst, x, y):
            pltpu.make_async_remote_copy(
                src_ref=src, dst_ref=dst, send_sem=halo_s.at[h, kind], recv_sem=halo_r.at[h, kind],
                device_id={"lon": x, "lat": y}).start()
        copy(2, al.at[fs, top, low], corners_i.at[0, fs], west, north)
        copy(2, al.at[fs, top, high], corners_i.at[1, fs], east, north)
        copy(2, al.at[fs, bottom, low], corners_i.at[2, fs], west, south)
        copy(2, al.at[fs, bottom, high], corners_i.at[3, fs], east, south)
        copy(0, strips_o.at[0, fs], strips_i.at[0, fs], east, lat)
        copy(0, strips_o.at[1, fs], strips_i.at[1, fs], west, lat)
        copy(1, al.at[fs, top, :], rows_i.at[0, fs], lon, north)
        copy(1, al.at[fs, bottom, :], rows_i.at[1, fs], lon, south)

    def wait_halo(h, f, n):
        fs = pl.ds(f, n)
        for kind, ref in enumerate((strips_i, rows_i, corners_i)):
            for sem in (halo_s, halo_r):
                pltpu.make_async_copy(ref.at[:, fs], ref.at[:, fs], sem.at[h, kind]).wait()

    def unpack_halo(f):
        outer = pl.ds(384, 128)
        from_w, from_e = strips_i[0, f], strips_i[1, f]
        for i in range(20):
            rows = pl.ds(i * 8, 8)
            e = pltpu.roll(from_e, 96 - 4 * i, 1) if i != 24 else from_e
            w = pltpu.roll(from_w, 124 - 4 * i, 1)
            al[f, rows, outer] = jnp.where(lane < 96, al[f, rows, outer], jnp.where(lane < 112, e, w))
        last = jnp.where(sub_w < 4, rows_i[0, f], rows_i[1, f])
        e = pltpu.roll(jnp.where(sub < 4, corners_i[0, f], corners_i[2, f]), 96, 1)
        w = pltpu.roll(jnp.where(sub < 4, corners_i[1, f], corners_i[3, f]), 32, 1)
        al[f, pl.ds(160, 8), pl.ds(0, 384)] = last[:, :384]
        al[f, pl.ds(160, 8), outer] = jnp.where(lane < 96, last[:, 384:], jnp.where(lane < 112, e, w))

    def rows_of(i):
        return pl.ds(i * 8, 8) if isinstance(i, int) else pl.ds(pl.multiple_of(i * 8, 8), 8)

    def around(i):
        return rows_of(i), rows_of((i + TILES - 1) % TILES if isinstance(i, int) else lax.rem(i + TILES - 1, TILES)), rows_of((i + 1) % TILES if isinstance(i, int) else lax.rem(i + 1, TILES))

    def up(c, p):
        return pltpu.roll(jnp.where(sub_w == 7, p, c), 1, 0)

    def down(c, n):
        return pltpu.roll(jnp.where(sub_w == 0, n, c), 7, 0)

    def to_east(c):
        return pltpu.roll(c, 511, 1)

    def to_west(c):
        return pltpu.roll(c, 1, 1)

    get_kmt.wait()
    get_kappa.wait()

    def widen(i, _):
        rows = rows_of(i)
        for t in range(4):
            w = min(128, COLS - t * 128)
            at = pl.ds(t * 128, w)
            al[KMT, rows, at] = levels[rows, at].astype(f32)
            al[KAPPA, rows, at] = kap[0, rows, at]
            al[KAPPA + 1, rows, at] = kap[1, rows, at]
        return 0
    for i in range(20):
        widen(i, 0)
    for f in (4, 5, 6):
        stage_strips(f)
    spread(ORDER[0])
    to_scalars.wait()
    pl.semaphore_wait(barrier, len(EVERY))
    start_halo(4, 4, 3)
    send_part(ORDER[0])
    for f in ORDER[1:]:
        spread(f)
        if f == ORDER[1]:
            send_part(f)

    wait_halo(4, 4, 3)
    for f in (4, 5, 6):
        unpack_halo(f)
    inside_s = (lat != NLAT - 1).astype(f32)
    inside_n = (lat != 0).astype(f32)
    edge = al[KMT, pl.ds(160, 8), :]
    al[KMT, pl.ds(160, 8), :] = jnp.where(sub_w < 4, edge * inside_s, edge * inside_n)

    def faces(i, _):
        here, prev, after = around(i)
        kc = al[KMT, here, :]
        ku, kd, ke = up(kc, al[KMT, prev, :]), down(kc, al[KMT, after, :]), to_east(kc)
        ku, kd, ke = jnp.minimum(kc, ku), jnp.minimum(kc, kd), jnp.minimum(kc, ke)
        for l in range(2):
            c = al[KAPPA + l, here, :]
            face[3 * l, here, :] = jnp.where(ke > l, 0.5 * (c + to_east(c)), 0.0)
            face[3 * l + 1, here, :] = jnp.where(ku > l, 0.5 * (c + up(c, al[KAPPA + l, prev, :])), 0.0)
            face[3 * l + 2, here, :] = jnp.where(kd > l, 0.5 * (c + down(c, al[KAPPA + l, after, :])), 0.0)
        col[here, :] = (kc > 0).astype(f32)
        dep[here, :] = (kc > 0).astype(f32) + 1.5 * (kc > 1).astype(f32)
        return 0
    for i in range(TILES):
        faces(i, 0)

    def place(f):
        level = float(f % 2)

        def band(by, _):
            code = [table[0, 32 + by * BX + bx] for bx in range(BX)]
            src = [c >> 1 for c in code]
            second = [jnp.full((8, 128), c & 1, i32) == 1 for c in code]
            for i in range(5):
                rows_out = pl.ds(by * BH + i * 8, 8)
                v = []
                for bx in range(BX):
                    a = landed[f][src[bx], pl.ds(i * 8, 8), :]
                    o = (BW * bx) % 128
                    direct = pltpu.roll(a, o, 1) if o else a
                    crossed = pltpu.roll(a, (o + 64) % 128, 1)
                    v.append(jnp.where(second[bx], crossed, direct))
                for t, (x, y, z, p, q) in enumerate(((0, 1, 2, 60, 120), (2, 3, 4, 52, 112), (4, 5, 6, 44, 104), (6, 7, 7, 36, 128))):
                    at = pl.ds(t * 128, 128)
                    w = jnp.where(lane < p, v[x], jnp.where(lane < q, v[y], v[z]))
                    al[f, rows_out, at] = jnp.where(al[KMT, rows_out, at] > level, w, 0.0)
            return 0
        for by in range(BY):
            band(by, 0)

    def diffuse(f, first):
        t, l = divmod(f, 2)
        dz = 1.0 + 0.5 * l

        def tile(i, store):
            here, prev, after = around(i)
            c = al[f, here, :]
            fe = face[3 * l, here, :] * (to_east(c) - c)
            change = fe - to_west(fe)
            change = change + face[3 * l + 1, here, :] * (up(c, al[f, prev, :]) - c)
            change = change + face[3 * l + 2, here, :] * (down(c, al[f, after, :]) - c)
            v = jnp.where(al[KMT, here, :] > float(l), c + change, 0.0)
            if store:
                for p in range(4):
                    w = min(128, COLS - p * 128)
                    fresh_t[t, l, here, pl.ds(p * 128, w)] = v[:, p * 128:p * 128 + w]
            share = (dz * haline) * v if t else (-dz) * (thermal * v + cabbeling * v * v)
            vs[0, here, :] = share if first else vs[0, here, :] + share

        def several(j, _):
            for d in range(20):
                tile(20 * j + d, True)
            return 0
        several(0, 0)
        tile(TILES - 1, False)

    for n, f in enumerate(ORDER):
        part_done(a2a_r, f).wait()
        place(f)
        stage_strips(f)
        start_halo(f, f, 1)
        if n < 2:
            send_part(ORDER[n + 2])
        if n:
            g = ORDER[n - 1]
            wait_halo(g, g, 1)
            unpack_halo(g)
            diffuse(g, n == 1)
    g = ORDER[3]
    wait_halo(g, g, 1)
    unpack_halo(g)
    diffuse(g, False)
    result = pltpu.make_async_copy(fresh_t, out_t, out_sem.at[0])
    result.start()

    sums = []
    for order in range(3):
        def apply(i, acc, order=order, add=True):
            here, prev, after = around(i)
            c = vs[order, here, :]
            m = up(c, vs[order, prev, :]) + down(c, vs[order, after, :])
            q = c + 0.5 * m
            v = dep[here, :] * c - col[here, :] * (to_east(q) + to_west(q) + m)
            if order < 2:
                vs[order + 1, here, :] = v
            return (acc[0] + c * c, acc[1] + c * v) if add else acc

        def several(j, acc, apply=apply):
            for d in range(20):
                acc = apply(20 * j + d, acc)
            return acc
        zero = jnp.zeros((8, 512), f32)
        acc = several(0, (zero, zero))
        if order < 2:
            apply(TILES - 1, acc, add=False)
        sums += list(acc)

    powers = pltpu.make_async_copy(vs, out_v, out_sem.at[2])
    powers.start()
    tile = jnp.zeros((8, 128), f32)
    for k, s in enumerate(sums):
        s = s[:, :128] + s[:, 128:256] + s[:, 256:384] + jnp.where(lane < 96, s[:, 384:], 0.0)
        tile = jnp.where(sub == k, jnp.sum(s, axis=0, keepdims=True), tile)
    tile = jnp.where(sub == lane, jnp.sum(tile, axis=1, keepdims=True), 0.0)
    mine = jnp.sum(tile, axis=0, keepdims=True)
    part[...] = mine
    for k, (x, y, z, c) in enumerate(EVERY):
        pltpu.make_async_remote_copy(
            src_ref=part, dst_ref=gathered.at[k], send_sem=red_s, recv_sem=red_r,
            device_id={"lon": xs[x] + ys[y], "lat": zs[z] + cs[c]}).start()
    pltpu.make_async_copy(gathered, gathered, red_r).wait()
    total = mine + jnp.sum(gathered[...], axis=0)
    summed[...] = total
    sums_out = pltpu.make_async_copy(summed, out_n, out_sem.at[1])
    sums_out.start()

    for f in ORDER:
        part_done(a2a_s, f).wait()
    pltpu.make_async_copy(gathered, gathered, red_s).wait()
    result.wait()
    powers.wait()
    sums_out.wait()


def finish(made_t, made_v, made_n, out_t, out_s, fresh_t, vs, summed, stream, in_sem, out_sem):
    get_sums = pltpu.make_async_copy(made_n, summed, in_sem.at[4])
    get_powers = pltpu.make_async_copy(made_v, vs, in_sem.at[5])
    cells = [(t, l) for t in range(2) for l in range(2)]
    ins = [pltpu.make_async_copy(made_t.at[t, l], fresh_t.at[t, l], in_sem.at[2 * t + l]) for t, l in cells]
    outs = [pltpu.make_async_copy(fresh_t.at[t, l], out_t.at[t, l], out_sem.at[2 * t + l]) for t, l in cells]
    for load in [get_sums] + ins + [get_powers]:
        load.start()
    for load, store in zip(ins, outs):
        load.wait()
        store.start()
    get_sums.wait()
    total = summed[...]
    nu = [total[:, k:k + 1] for k in range(6)]

    def dot(a, b):
        total = None
        for i, x in enumerate(a):
            for j, y in enumerate(b):
                term = x * y * nu[i + j]
                total = term if total is None else total + term
        return total

    def image(a):
        return [SHIFT * a[0]] + [SHIFT * a[k] + a[k - 1] for k in range(1, len(a))] + [a[-1]]

    unit = jnp.ones((1, 1), f32)
    x = []
    res, direct, norm = [unit], [unit], nu[0]
    for k in range(3):
        img = image(direct)
        alpha = norm / dot(direct, img)
        x = [(x[n] + alpha * d) if n < len(x) else alpha * d for n, d in enumerate(direct)]
        if k < 2:
            res = [(res[n] - alpha * d) if n < len(res) else -alpha * d for n, d in enumerate(img)]
            later = dot(res, res)
            beta = later / norm
            direct = [(res[n] + beta * direct[n]) if n < len(direct) else res[n] for n in range(len(res))]
            norm = later

    c0, c1, c2 = (jnp.broadcast_to(v, (8, 128)) for v in x)
    get_powers.wait()
    for i in range(20):
        rows = pl.ds(i * 8, 8)
        for t in range(4):
            w = min(128, COLS - t * 128)
            at = pl.ds(t * 128, 128)
            v = c0 * vs[0, rows, at] + c1 * vs[1, rows, at] + c2 * vs[2, rows, at]
            stream[rows, pl.ds(t * 128, w)] = v[:, :w]
    final = pltpu.make_async_copy(stream, out_s, out_sem.at[4])
    final.start()
    for store in outs:
        store.wait()
    final.wait()


def body(checkpoint, slot_dest, kmt, kappa):
    sem = pltpu.SemaphoreType.DMA
    vm = pltpu.VMEM
    made = pl.pallas_call(
        kernel,
        out_shape=(
            jax.ShapeDtypeStruct((2, 2, ROWS, COLS), f32),
            jax.ShapeDtypeStruct((3, WIDE, 512), f32),
            jax.ShapeDtypeStruct((1, 128), f32),
        ),
        in_specs=[pl.BlockSpec(memory_space=pl.ANY)] * 4,
        out_specs=[pl.BlockSpec(memory_space=pl.ANY)] * 3,
        scratch_shapes=[
            vm((Q, 9600), f32),
            vm((1, NLON * Q), i32),
            vm((1, 128), i32),
            pltpu.SMEM((1, 128), i32),
            vm((4, Q, BH, 128), f32),
            vm((4, NLON - 1, BH, 128), f32),
            *[vm((NLON, BH, 128), f32)] * 4,
            vm((ROWS, COLS), i32),
            vm((2, ROWS, COLS), f32),
            vm((7, WIDE, 512), f32),
            vm((6, WIDE, 512), f32),
            vm((2, 7, 8, 128), f32),
            vm((2, 7, 8, 128), f32),
            vm((2, 7, 8, 512), f32),
            vm((4, 7, 8, 128), f32),
            vm((3, WIDE, 512), f32),
            vm((WIDE, 512), f32),
            vm((WIDE, 512), f32),
            vm((2, 2, ROWS, COLS), f32),
            vm((1, 128), f32),
            vm((1, 128), f32),
            vm((NLON * NLAT - 1, 1, 128), f32),
            sem((5,)),
            sem((3,)),
            sem((4,)),
            sem((4,)),
            sem((5, 3)),
            sem((5, 3)),
            sem,
            sem,
        ],
        compiler_params=pltpu.CompilerParams(collective_id=0, has_side_effects=True, vmem_limit_bytes=60 << 20),
    )(checkpoint[0], slot_dest, kmt, kappa)
    return pl.pallas_call(
        finish,
        out_shape=(jax.ShapeDtypeStruct((2, 2, ROWS, COLS), f32), jax.ShapeDtypeStruct((ROWS, COLS), f32)),
        in_specs=[pl.BlockSpec(memory_space=pl.ANY)] * 3,
        out_specs=[pl.BlockSpec(memory_space=pl.ANY)] * 2,
        scratch_shapes=[
            vm((2, 2, ROWS, COLS), f32),
            vm((3, WIDE, 512), f32),
            vm((1, 128), f32),
            vm((ROWS, COLS), f32),
            sem((6,)),
            sem((5,)),
        ],
        compiler_params=pltpu.CompilerParams(vmem_limit_bytes=60 << 20),
    )(*made)


def solution(mesh):
    placed = (P("lat", "lon", None), P("lat", None), P("lat", "lon"), P(None, "lat", "lon"))
    return jax.shard_map(
        body,
        mesh=mesh,
        in_specs=placed,
        out_specs=(P(None, None, "lat", "lon"), P("lat", "lon")),
        check_vma=False,
    )
```

```python
import jax
import jax.numpy as jnp
from jax import lax
from jax.experimental import pallas as pl
from jax.experimental.pallas import tpu as pltpu
from jax.sharding import PartitionSpec as P

BW = 60
BH = 40
BX = 8
BY = 4
Q = 32
ROWS = 160
COLS = 480
NLON = 16
NLAT = 8
SIDE = 4
TILES = 21
WIDE = TILES * 8
PART = BH * BW
SHIFT = 6.0
ORDER = (0, 2, 1, 3)
KAPPA, KMT = 4, 6

thermal = 0.25
haline = 0.75
cabbeling = 0.05

f32 = jnp.float32
i32 = jnp.int32


def hops(step):
    return (0, 1, 2, 1)[step]


BAND = [(0, 1), (2, 2), (1, 0), (2, 1), (0, 3), (1, 2), (3, 0), (2, 3), (1, 1), (3, 2), (3, 3), (0, 2), (1, 3), (2, 0), (3, 1)]
EVERY = sorted(
    [(x, y, z, c) for x in range(4) for y in range(4) for z in range(4) for c in range(2) if x or y or z or c],
    key=lambda k: -(hops(k[0]) + hops(k[1]) + hops(k[2])),
)


def kernel(ckpt, dest, kmt, kappa, out_t, out_v, out_n,
           blocks, slots, row, table, parted, packed0, packed1, packed2, packed3, landed0, landed1, landed2, landed3, levels, kap, al, face,
           strips_o, strips_i, rows_i, corners_i,
           vs, col, dep, fresh_t, part, summed, gathered,
           in_sem, out_sem, a2a_s, a2a_r, halo_s, halo_r, red_s, red_r):
    lon = lax.axis_index("lon")
    lat = lax.axis_index("lat")
    packed = (packed0, packed1, packed2, packed3)
    landed = (landed0, landed1, landed2, landed3)
    xs = [lax.rem(lon // SIDE + d, SIDE) * SIDE for d in range(4)]
    ys = [lax.rem(lax.rem(lon, SIDE) + d, SIDE) for d in range(4)]
    zs = [lax.rem(lat // 2 + d, 4) * 2 for d in range(4)]
    cs = [lax.rem(lat + d, 2) for d in range(2)]
    east, west = lax.rem(lon + 1, NLON), lax.rem(lon + NLON - 1, NLON)
    south, north = lax.rem(lat + 1, NLAT), lax.rem(lat + NLAT - 1, NLAT)

    get_slots = pltpu.make_async_copy(dest, slots, in_sem.at[0])
    get_blocks = pltpu.make_async_copy(ckpt, blocks, in_sem.at[1])
    get_kmt = pltpu.make_async_copy(kmt, levels, in_sem.at[2])
    get_kappa = pltpu.make_async_copy(kappa, kap, in_sem.at[3])
    for load in (get_slots, get_blocks, get_kmt, get_kappa):
        load.start()

    barrier = pltpu.get_barrier_semaphore()
    for x, y, z, c in EVERY:
        pl.semaphore_signal(barrier, inc=1, device_id={"lon": xs[x] + ys[y], "lat": zs[z] + cs[c]})

    lane = lax.broadcasted_iota(i32, (8, 128), 1)
    sub = lax.broadcasted_iota(i32, (8, 128), 0)
    lane32 = lax.broadcasted_iota(i32, (32, 128), 1)
    lane40 = lax.broadcasted_iota(i32, (BH, 128), 1)
    sub_w = lax.broadcasted_iota(i32, (8, 512), 0)

    get_slots.wait()
    dst = slots[...]
    owner = dst >> 5
    at = lax.broadcasted_iota(i32, (1, NLON * Q), 1)
    source, slot = at >> 5, at & 31
    line = lax.broadcasted_iota(i32, (8, NLON * Q), 0)
    count = (owner == jnp.where(line == 0, lon, jnp.where(line == 1, east, west))).astype(i32)
    slot_8 = lax.broadcasted_iota(i32, (8, NLON * Q), 1) & 31
    for d in (1, 2, 4, 8, 16):
        count = count + jnp.where(slot_8 >= d, pltpu.roll(count, d, 1), 0)
    code, code_e, code_w = (2 * source + jnp.clip(count[k:k + 1] - 1, 0, 1) for k in range(3))
    position = lax.broadcasted_iota(i32, (Q, NLON * Q), 0)
    found = jnp.max(jnp.where(dst == lon * Q + position, code, 0), axis=1, keepdims=True)
    beside = jnp.where(line < 4, east * Q + line * BX, west * Q + (line - 4) * BX + BX - 1)
    sides = jnp.max(jnp.where(dst == beside, jnp.where(line < 4, code_e, code_w), 0), axis=1, keepdims=True)
    to = jnp.where(source == lon, owner, -1) == lax.broadcasted_iota(i32, (NLON, NLON * Q), 0)
    one = jnp.min(jnp.where(to, slot, Q - 1), axis=1, keepdims=True)
    two = jnp.max(jnp.where(to, slot, 0), axis=1, keepdims=True)
    entries = jnp.concatenate([one, two, found, sides], axis=0)
    diagonal = lax.broadcasted_iota(i32, (72, 128), 0) == lax.broadcasted_iota(i32, (72, 128), 1)
    row[...] = jnp.sum(jnp.where(diagonal, entries, 0), axis=0, keepdims=True)
    to_scalars = pltpu.make_async_copy(row, table, in_sem.at[4])
    to_scalars.start()

    get_blocks.wait()

    def spread(f):
        flat = parted.at[f].reshape(Q * BH, 128)
        for r in range(BH):
            q, l = divmod(f * PART + r * BW, 128)
            a = blocks[:, pl.ds(q * 128, 128)]
            if l:
                a = pltpu.roll(a, 128 - l, 1)
            if l + BW > 128:
                b = blocks[:, pl.ds(q * 128 + 128, 128)]
                a = jnp.where(lane32 < 128 - l, a, pltpu.roll(b, 128 - l, 1))
            flat[pl.ds(r, Q, stride=BH), :] = a

    def pack(f, e):
        a = parted[f, table[0, e]]
        b = parted[f, table[0, NLON + e]]
        return jnp.where(lane40 < 64, a, pltpu.roll(b, 64, 1))

    def pack_sides(f, e):
        e_east, e_west = lax.rem(e + 1, NLON), lax.rem(e + NLON - 1, NLON)
        picks = [(table[0, e_east], 0), (table[0, NLON + e_east], 0), (table[0, e_west], 56), (table[0, NLON + e_west], 56)]
        acc = None
        for i in range(5):
            for n, (j, start) in enumerate(picks):
                pos = 16 * i + 4 * n
                v = parted[f, j, pl.ds(i * 8, 8), :]
                move = (pos - start) % 128
                v = pltpu.roll(v, move, 1) if move else v
                acc = v if acc is None else jnp.where(lane >= pos, v, acc)
        return acc

    def send_part(f):
        inner = pl.ds(0, BH)
        for k, (x, y) in enumerate(BAND):
            e = jnp.where(cs[0] == 0, xs[x] + ys[y], xs[y] + ys[x])
            packed[f][k, inner, :] = pack(f, e)
            if f == ORDER[3]:
                packed[f][k, pl.ds(BH, 8), :] = pack_sides(f, e)
            pltpu.make_async_remote_copy(
                src_ref=packed[f].at[k], dst_ref=landed[f].at[lon], send_sem=a2a_s.at[f], recv_sem=a2a_r.at[f],
                device_id={"lon": e, "lat": lat}).start()
        landed[f][lon, inner, :] = pack(f, lon)
        if f == ORDER[3]:
            landed[f][lon, pl.ds(BH, 8), :] = pack_sides(f, lon)

    def part_done(sem, f):
        most = landed[f].at[pl.ds(0, NLON - 1)]
        return pltpu.make_async_copy(most, most, sem.at[f])

    def stage_strips(f):
        for side, tile, start in ((0, 3, 92), (1, 0, 0)):
            acc = None
            for i in range(20):
                move = (4 * i - start) % 128
                v = al[f, pl.ds(i * 8, 8), pl.ds(tile * 128, 128)]
                v = pltpu.roll(v, move, 1) if move else v
                acc = v if acc is None else jnp.where(lane >= 4 * i, v, acc)
            strips_o[side, f] = acc

    def start_halo(h, f, n):
        fs = pl.ds(f, n)
        top, bottom, low, high = pl.ds(0, 8), pl.ds(152, 8), pl.ds(0, 128), pl.ds(384, 128)

        def copy(kind, src, dst, x, y):
            pltpu.make_async_remote_copy(
                src_ref=src, dst_ref=dst, send_sem=halo_s.at[h, kind], recv_sem=halo_r.at[h, kind],
                device_id={"lon": x, "lat": y}).start()
        copy(2, al.at[fs, top, low], corners_i.at[0, fs], west, north)
        copy(2, al.at[fs, top, high], corners_i.at[1, fs], east, north)
        copy(2, al.at[fs, bottom, low], corners_i.at[2, fs], west, south)
        copy(2, al.at[fs, bottom, high], corners_i.at[3, fs], east, south)
        copy(0, strips_o.at[0, fs], strips_i.at[0, fs], east, lat)
        copy(0, strips_o.at[1, fs], strips_i.at[1, fs], west, lat)
        copy(1, al.at[fs, top, :], rows_i.at[0, fs], lon, north)
        copy(1, al.at[fs, bottom, :], rows_i.at[1, fs], lon, south)

    def wait_halo(h, f, n):
        fs = pl.ds(f, n)
        for kind, ref in enumerate((strips_i, rows_i, corners_i)):
            for sem in (halo_s, halo_r):
                pltpu.make_async_copy(ref.at[:, fs], ref.at[:, fs], sem.at[h, kind]).wait()

    def unpack_halo(f):
        outer = pl.ds(384, 128)
        from_w, from_e = strips_i[0, f], strips_i[1, f]
        for i in range(20):
            rows = pl.ds(i * 8, 8)
            e = pltpu.roll(from_e, 96 - 4 * i, 1) if i != 24 else from_e
            w = pltpu.roll(from_w, 124 - 4 * i, 1)
            al[f, rows, outer] = jnp.where(lane < 96, al[f, rows, outer], jnp.where(lane < 112, e, w))
        last = jnp.where(sub_w < 4, rows_i[0, f], rows_i[1, f])
        e = pltpu.roll(jnp.where(sub < 4, corners_i[0, f], corners_i[2, f]), 96, 1)
        w = pltpu.roll(jnp.where(sub < 4, corners_i[1, f], corners_i[3, f]), 32, 1)
        al[f, pl.ds(160, 8), pl.ds(0, 384)] = last[:, :384]
        al[f, pl.ds(160, 8), outer] = jnp.where(lane < 96, last[:, 384:], jnp.where(lane < 112, e, w))

    def rows_of(i):
        return pl.ds(i * 8, 8) if isinstance(i, int) else pl.ds(pl.multiple_of(i * 8, 8), 8)

    def around(i):
        return rows_of(i), rows_of((i + TILES - 1) % TILES if isinstance(i, int) else lax.rem(i + TILES - 1, TILES)), rows_of((i + 1) % TILES if isinstance(i, int) else lax.rem(i + 1, TILES))

    def up(c, p):
        return pltpu.roll(jnp.where(sub_w == 7, p, c), 1, 0)

    def down(c, n):
        return pltpu.roll(jnp.where(sub_w == 0, n, c), 7, 0)

    def to_east(c):
        return pltpu.roll(c, 511, 1)

    def to_west(c):
        return pltpu.roll(c, 1, 1)

    get_kmt.wait()
    get_kappa.wait()

    def widen(i, _):
        rows = rows_of(i)
        for t in range(4):
            w = min(128, COLS - t * 128)
            at = pl.ds(t * 128, w)
            al[KMT, rows, at] = levels[rows, at].astype(f32)
            al[KAPPA, rows, at] = kap[0, rows, at]
            al[KAPPA + 1, rows, at] = kap[1, rows, at]
        return 0
    for i in range(20):
        widen(i, 0)
    for f in (4, 5, 6):
        stage_strips(f)
    spread(ORDER[0])
    to_scalars.wait()
    pl.semaphore_wait(barrier, len(EVERY))
    start_halo(4, 4, 3)
    send_part(ORDER[0])
    for f in ORDER[1:]:
        spread(f)
        if f == ORDER[1]:
            send_part(f)

    wait_halo(4, 4, 3)
    for f in (4, 5, 6):
        unpack_halo(f)
    inside_s = (lat != NLAT - 1).astype(f32)
    inside_n = (lat != 0).astype(f32)
    edge = al[KMT, pl.ds(160, 8), :]
    al[KMT, pl.ds(160, 8), :] = jnp.where(sub_w < 4, edge * inside_s, edge * inside_n)

    def faces(i, _):
        here, prev, after = around(i)
        kc = al[KMT, here, :]
        ku, kd, ke = up(kc, al[KMT, prev, :]), down(kc, al[KMT, after, :]), to_east(kc)
        ku, kd, ke = jnp.minimum(kc, ku), jnp.minimum(kc, kd), jnp.minimum(kc, ke)
        for l in range(2):
            c = al[KAPPA + l, here, :]
            face[3 * l, here, :] = jnp.where(ke > l, 0.5 * (c + to_east(c)), 0.0)
            face[3 * l + 1, here, :] = jnp.where(ku > l, 0.5 * (c + up(c, al[KAPPA + l, prev, :])), 0.0)
            face[3 * l + 2, here, :] = jnp.where(kd > l, 0.5 * (c + down(c, al[KAPPA + l, after, :])), 0.0)
        col[here, :] = (kc > 0).astype(f32)
        dep[here, :] = (kc > 0).astype(f32) + 1.5 * (kc > 1).astype(f32)
        return 0
    for i in range(TILES):
        faces(i, 0)

    def place(f):
        level = float(f % 2)

        def band(by, _):
            code = [table[0, 32 + by * BX + bx] for bx in range(BX)]
            src = [c >> 1 for c in code]
            second = [jnp.full((8, 128), c & 1, i32) == 1 for c in code]
            for i in range(5):
                rows_out = pl.ds(by * BH + i * 8, 8)
                v = []
                for bx in range(BX):
                    a = landed[f][src[bx], pl.ds(i * 8, 8), :]
                    o = (BW * bx) % 128
                    direct = pltpu.roll(a, o, 1) if o else a
                    crossed = pltpu.roll(a, (o + 64) % 128, 1)
                    v.append(jnp.where(second[bx], crossed, direct))
                for t, (x, y, z, p, q) in enumerate(((0, 1, 2, 60, 120), (2, 3, 4, 52, 112), (4, 5, 6, 44, 104), (6, 7, 7, 36, 128))):
                    at = pl.ds(t * 128, 128)
                    w = jnp.where(lane < p, v[x], jnp.where(lane < q, v[y], v[z]))
                    al[f, rows_out, at] = jnp.where(al[KMT, rows_out, at] > level, w, 0.0)
            return 0
        for by in range(BY):
            band(by, 0)

    def place_sides(f):
        level = float(f % 2)
        outer = pl.ds(384, 128)
        for by in range(BY):
            both = []
            for n in range(2):
                code = table[0, 64 + 4 * n + by]
                v = landed[f][code >> 1, pl.ds(BH, 8), :]
                both.append(jnp.where(jnp.full((8, 128), code & 1, i32) == 1, pltpu.roll(v, 124, 1), v))
            for i in range(5):
                rows = pl.ds(by * BH + i * 8, 8)
                e = pltpu.roll(both[0], 96 - 16 * i, 1)
                w = pltpu.roll(both[1], 116 - 16 * i, 1)
                v = jnp.where(al[KMT, rows, outer] > level, jnp.where(lane < 112, e, w), 0.0)
                al[f, rows, outer] = jnp.where(lane < 96, al[f, rows, outer], v)

    def row_copies(f):
        return [
            pltpu.make_async_remote_copy(
                src_ref=al.at[f, pl.ds(start, 8), :], dst_ref=rows_i.at[n, f], send_sem=halo_s.at[f, n], recv_sem=halo_r.at[f, n],
                device_id={"lon": lon, "lat": to})
            for n, (start, to) in enumerate(((0, north), (152, south)))
        ]

    def diffuse(f, first):
        t, l = divmod(f, 2)
        dz = 1.0 + 0.5 * l

        def tile(i, store):
            here, prev, after = around(i)
            c = al[f, here, :]
            fe = face[3 * l, here, :] * (to_east(c) - c)
            change = fe - to_west(fe)
            change = change + face[3 * l + 1, here, :] * (up(c, al[f, prev, :]) - c)
            change = change + face[3 * l + 2, here, :] * (down(c, al[f, after, :]) - c)
            v = jnp.where(al[KMT, here, :] > float(l), c + change, 0.0)
            if store:
                for p in range(4):
                    w = min(128, COLS - p * 128)
                    fresh_t[t, l, here, pl.ds(p * 128, w)] = v[:, p * 128:p * 128 + w]
            share = (dz * haline) * v if t else (-dz) * (thermal * v + cabbeling * v * v)
            vs[0, here, :] = share if first else vs[0, here, :] + share

        def several(j, _):
            for d in range(20):
                tile(20 * j + d, True)
            return 0
        several(0, 0)
        tile(TILES - 1, False)

    for n, f in enumerate(ORDER):
        part_done(a2a_r, f).wait()
        if n < 2:
            send_part(ORDER[n + 2])
        place(f)
        if n < 3:
            stage_strips(f)
            start_halo(f, f, 1)
        else:
            place_sides(f)
            last = row_copies(f)
            for c in last:
                c.start()
        if n >= 2:
            g = ORDER[n - 2]
            wait_halo(g, g, 1)
            unpack_halo(g)
            diffuse(g, n == 2)
    wait_halo(ORDER[2], ORDER[2], 1)
    unpack_halo(ORDER[2])
    diffuse(ORDER[2], False)
    for c in last:
        c.wait()
    f = ORDER[3]
    al[f, pl.ds(160, 8), :] = jnp.where(sub_w < 4, rows_i[0, f], rows_i[1, f])
    diffuse(f, False)
    result = pltpu.make_async_copy(fresh_t, out_t, out_sem.at[0])
    result.start()

    sums = []
    for order in range(3):
        def apply(i, acc, order=order, add=True):
            here, prev, after = around(i)
            c = vs[order, here, :]
            m = up(c, vs[order, prev, :]) + down(c, vs[order, after, :])
            q = c + 0.5 * m
            v = dep[here, :] * c - col[here, :] * (to_east(q) + to_west(q) + m)
            if order < 2:
                vs[order + 1, here, :] = v
            return (acc[0] + c * c, acc[1] + c * v) if add else acc

        def several(j, acc, apply=apply):
            for d in range(20):
                acc = apply(20 * j + d, acc)
            return acc
        zero = jnp.zeros((8, 512), f32)
        acc = several(0, (zero, zero))
        if order < 2:
            apply(TILES - 1, acc, add=False)
        sums += list(acc)

    powers = pltpu.make_async_copy(vs, out_v, out_sem.at[2])
    powers.start()
    tile = jnp.zeros((8, 128), f32)
    for k, s in enumerate(sums):
        s = s[:, :128] + s[:, 128:256] + s[:, 256:384] + jnp.where(lane < 96, s[:, 384:], 0.0)
        tile = jnp.where(sub == k, jnp.sum(s, axis=0, keepdims=True), tile)
    tile = jnp.where(sub == lane, jnp.sum(tile, axis=1, keepdims=True), 0.0)
    mine = jnp.sum(tile, axis=0, keepdims=True)
    part[...] = mine
    for k, (x, y, z, c) in enumerate(EVERY):
        pltpu.make_async_remote_copy(
            src_ref=part, dst_ref=gathered.at[k], send_sem=red_s, recv_sem=red_r,
            device_id={"lon": xs[x] + ys[y], "lat": zs[z] + cs[c]}).start()
    pltpu.make_async_copy(gathered, gathered, red_r).wait()
    total = mine + jnp.sum(gathered[...], axis=0)
    summed[...] = total
    sums_out = pltpu.make_async_copy(summed, out_n, out_sem.at[1])
    sums_out.start()

    for f in ORDER:
        part_done(a2a_s, f).wait()
    pltpu.make_async_copy(gathered, gathered, red_s).wait()
    result.wait()
    powers.wait()
    sums_out.wait()


def finish(made_t, made_v, made_n, out_t, out_s, fresh_t, vs, summed, stream, in_sem, out_sem):
    get_sums = pltpu.make_async_copy(made_n, summed, in_sem.at[4])
    get_powers = pltpu.make_async_copy(made_v, vs, in_sem.at[5])
    cells = [(t, l) for t in range(2) for l in range(2)]
    ins = [pltpu.make_async_copy(made_t.at[t, l], fresh_t.at[t, l], in_sem.at[2 * t + l]) for t, l in cells]
    outs = [pltpu.make_async_copy(fresh_t.at[t, l], out_t.at[t, l], out_sem.at[2 * t + l]) for t, l in cells]
    for load in [get_sums] + ins + [get_powers]:
        load.start()
    for load, store in zip(ins, outs):
        load.wait()
        store.start()
    get_sums.wait()
    total = summed[...]
    nu = [total[:, k:k + 1] for k in range(6)]

    def dot(a, b):
        total = None
        for i, x in enumerate(a):
            for j, y in enumerate(b):
                term = x * y * nu[i + j]
                total = term if total is None else total + term
        return total

    def image(a):
        return [SHIFT * a[0]] + [SHIFT * a[k] + a[k - 1] for k in range(1, len(a))] + [a[-1]]

    unit = jnp.ones((1, 1), f32)
    x = []
    res, direct, norm = [unit], [unit], nu[0]
    for k in range(3):
        img = image(direct)
        alpha = norm / dot(direct, img)
        x = [(x[n] + alpha * d) if n < len(x) else alpha * d for n, d in enumerate(direct)]
        if k < 2:
            res = [(res[n] - alpha * d) if n < len(res) else -alpha * d for n, d in enumerate(img)]
            later = dot(res, res)
            beta = later / norm
            direct = [(res[n] + beta * direct[n]) if n < len(direct) else res[n] for n in range(len(res))]
            norm = later

    c0, c1, c2 = (jnp.broadcast_to(v, (8, 128)) for v in x)
    get_powers.wait()
    for i in range(20):
        rows = pl.ds(i * 8, 8)
        for t in range(4):
            w = min(128, COLS - t * 128)
            at = pl.ds(t * 128, 128)
            v = c0 * vs[0, rows, at] + c1 * vs[1, rows, at] + c2 * vs[2, rows, at]
            stream[rows, pl.ds(t * 128, w)] = v[:, :w]
    final = pltpu.make_async_copy(stream, out_s, out_sem.at[4])
    final.start()
    for store in outs:
        store.wait()
    final.wait()


def body(checkpoint, slot_dest, kmt, kappa):
    sem = pltpu.SemaphoreType.DMA
    vm = pltpu.VMEM
    made = pl.pallas_call(
        kernel,
        out_shape=(
            jax.ShapeDtypeStruct((2, 2, ROWS, COLS), f32),
            jax.ShapeDtypeStruct((3, WIDE, 512), f32),
            jax.ShapeDtypeStruct((1, 128), f32),
        ),
        in_specs=[pl.BlockSpec(memory_space=pl.ANY)] * 4,
        out_specs=[pl.BlockSpec(memory_space=pl.ANY)] * 3,
        scratch_shapes=[
            vm((Q, 9600), f32),
            vm((1, NLON * Q), i32),
            vm((1, 128), i32),
            pltpu.SMEM((1, 128), i32),
            vm((4, Q, BH, 128), f32),
            *[vm((NLON - 1, BH, 128), f32)] * 3,
            vm((NLON - 1, BH + 8, 128), f32),
            *[vm((NLON, BH, 128), f32)] * 3,
            vm((NLON, BH + 8, 128), f32),
            vm((ROWS, COLS), i32),
            vm((2, ROWS, COLS), f32),
            vm((7, WIDE, 512), f32),
            vm((6, WIDE, 512), f32),
            vm((2, 7, 8, 128), f32),
            vm((2, 7, 8, 128), f32),
            vm((2, 7, 8, 512), f32),
            vm((4, 7, 8, 128), f32),
            vm((3, WIDE, 512), f32),
            vm((WIDE, 512), f32),
            vm((WIDE, 512), f32),
            vm((2, 2, ROWS, COLS), f32),
            vm((1, 128), f32),
            vm((1, 128), f32),
            vm((NLON * NLAT - 1, 1, 128), f32),
            sem((5,)),
            sem((3,)),
            sem((4,)),
            sem((4,)),
            sem((5, 3)),
            sem((5, 3)),
            sem,
            sem,
        ],
        compiler_params=pltpu.CompilerParams(collective_id=0, has_side_effects=True, vmem_limit_bytes=60 << 20),
    )(checkpoint[0], slot_dest, kmt, kappa)
    return pl.pallas_call(
        finish,
        out_shape=(jax.ShapeDtypeStruct((2, 2, ROWS, COLS), f32), jax.ShapeDtypeStruct((ROWS, COLS), f32)),
        in_specs=[pl.BlockSpec(memory_space=pl.ANY)] * 3,
        out_specs=[pl.BlockSpec(memory_space=pl.ANY)] * 2,
        scratch_shapes=[
            vm((2, 2, ROWS, COLS), f32),
            vm((3, WIDE, 512), f32),
            vm((1, 128), f32),
            vm((ROWS, COLS), f32),
            sem((6,)),
            sem((5,)),
        ],
        compiler_params=pltpu.CompilerParams(vmem_limit_bytes=60 << 20),
    )(*made)


def solution(mesh):
    placed = (P("lat", "lon", None), P("lat", None), P("lat", "lon"), P(None, "lat", "lon"))
    return jax.shard_map(
        body,
        mesh=mesh,
        in_specs=placed,
        out_specs=(P(None, None, "lat", "lon"), P("lat", "lon")),
        check_vma=False,
    )
```

```python
import jax
import jax.numpy as jnp
from jax import lax
from jax.experimental import pallas as pl
from jax.experimental.pallas import tpu as pltpu
from jax.sharding import PartitionSpec as P

BW = 60
BH = 40
BX = 8
BY = 4
Q = 32
ROWS = 160
COLS = 480
NLON = 16
NLAT = 8
SIDE = 4
TILES = 21
WIDE = TILES * 8
PART = BH * BW
SHIFT = 6.0
ORDER = (0, 2, 1, 3)
KAPPA, KMT = 4, 6

thermal = 0.25
haline = 0.75
cabbeling = 0.05

f32 = jnp.float32
i32 = jnp.int32


def hops(step):
    return (0, 1, 2, 1)[step]


BAND = [(1, 0), (2, 1), (0, 1), (1, 2), (3, 0), (2, 3), (0, 3), (3, 2), (1, 1), (2, 2), (3, 3), (2, 0), (1, 3), (0, 2), (3, 1)]
EVERY = sorted(
    [(x, y, z, c) for x in range(4) for y in range(4) for z in range(4) for c in range(2) if x or y or z or c],
    key=lambda k: -(hops(k[0]) + hops(k[1]) + hops(k[2])),
)


def kernel(ckpt, dest, kmt, kappa, out_t, out_v, out_n,
           blocks, slots, row, table, parted, packed0, packed1, packed2, packed3, landed0, landed1, landed2, landed3, levels, kap, al, face,
           strips_o, strips_i, rows_i, corners_i,
           vs, col, dep, fresh_t, part, summed, gathered,
           in_sem, out_sem, a2a_s, a2a_r, halo_s, halo_r, red_s, red_r):
    lon = lax.axis_index("lon")
    lat = lax.axis_index("lat")
    packed = (packed0, packed1, packed2, packed3)
    landed = (landed0, landed1, landed2, landed3)
    xs = [lax.rem(lon // SIDE + d, SIDE) * SIDE for d in range(4)]
    ys = [lax.rem(lax.rem(lon, SIDE) + d, SIDE) for d in range(4)]
    zs = [lax.rem(lat // 2 + d, 4) * 2 for d in range(4)]
    cs = [lax.rem(lat + d, 2) for d in range(2)]
    east, west = lax.rem(lon + 1, NLON), lax.rem(lon + NLON - 1, NLON)
    south, north = lax.rem(lat + 1, NLAT), lax.rem(lat + NLAT - 1, NLAT)

    get_slots = pltpu.make_async_copy(dest, slots, in_sem.at[0])
    get_blocks = pltpu.make_async_copy(ckpt, blocks, in_sem.at[1])
    get_kmt = pltpu.make_async_copy(kmt, levels, in_sem.at[2])
    get_kappa = pltpu.make_async_copy(kappa, kap, in_sem.at[3])
    for load in (get_slots, get_blocks, get_kmt, get_kappa):
        load.start()

    barrier = pltpu.get_barrier_semaphore()
    for x, y, z, c in EVERY:
        pl.semaphore_signal(barrier, inc=1, device_id={"lon": xs[x] + ys[y], "lat": zs[z] + cs[c]})

    lane = lax.broadcasted_iota(i32, (8, 128), 1)
    sub = lax.broadcasted_iota(i32, (8, 128), 0)
    lane32 = lax.broadcasted_iota(i32, (32, 128), 1)
    lane40 = lax.broadcasted_iota(i32, (BH, 128), 1)
    sub_w = lax.broadcasted_iota(i32, (8, 512), 0)

    get_slots.wait()
    dst = slots[...]
    owner = dst >> 5
    at = lax.broadcasted_iota(i32, (1, NLON * Q), 1)
    source, slot = at >> 5, at & 31
    line = lax.broadcasted_iota(i32, (8, NLON * Q), 0)
    count = (owner == jnp.where(line == 0, lon, jnp.where(line == 1, east, west))).astype(i32)
    slot_8 = lax.broadcasted_iota(i32, (8, NLON * Q), 1) & 31
    for d in (1, 2, 4, 8, 16):
        count = count + jnp.where(slot_8 >= d, pltpu.roll(count, d, 1), 0)
    code, code_e, code_w = (2 * source + jnp.clip(count[k:k + 1] - 1, 0, 1) for k in range(3))
    position = lax.broadcasted_iota(i32, (Q, NLON * Q), 0)
    found = jnp.max(jnp.where(dst == lon * Q + position, code, 0), axis=1, keepdims=True)
    beside = jnp.where(line < 4, east * Q + line * BX, west * Q + (line - 4) * BX + BX - 1)
    sides = jnp.max(jnp.where(dst == beside, jnp.where(line < 4, code_e, code_w), 0), axis=1, keepdims=True)
    to = jnp.where(source == lon, owner, -1) == lax.broadcasted_iota(i32, (NLON, NLON * Q), 0)
    one = jnp.min(jnp.where(to, slot, Q - 1), axis=1, keepdims=True)
    two = jnp.max(jnp.where(to, slot, 0), axis=1, keepdims=True)
    entries = jnp.concatenate([one, two, found, sides], axis=0)
    diagonal = lax.broadcasted_iota(i32, (72, 128), 0) == lax.broadcasted_iota(i32, (72, 128), 1)
    row[...] = jnp.sum(jnp.where(diagonal, entries, 0), axis=0, keepdims=True)
    to_scalars = pltpu.make_async_copy(row, table, in_sem.at[4])
    to_scalars.start()

    get_blocks.wait()

    def spread(f):
        flat = parted.at[f].reshape(Q * BH, 128)
        for r in range(BH):
            q, l = divmod(f * PART + r * BW, 128)
            a = blocks[:, pl.ds(q * 128, 128)]
            if l:
                a = pltpu.roll(a, 128 - l, 1)
            if l + BW > 128:
                b = blocks[:, pl.ds(q * 128 + 128, 128)]
                a = jnp.where(lane32 < 128 - l, a, pltpu.roll(b, 128 - l, 1))
            flat[pl.ds(r, Q, stride=BH), :] = a

    def pack(f, e):
        a = parted[f, table[0, e]]
        b = parted[f, table[0, NLON + e]]
        return jnp.where(lane40 < 64, a, pltpu.roll(b, 64, 1))

    def pack_sides(f, e):
        e_east, e_west = lax.rem(e + 1, NLON), lax.rem(e + NLON - 1, NLON)
        picks = [(table[0, e_east], 0), (table[0, NLON + e_east], 0), (table[0, e_west], 56), (table[0, NLON + e_west], 56)]
        acc = None
        for i in range(5):
            for n, (j, start) in enumerate(picks):
                pos = 16 * i + 4 * n
                v = parted[f, j, pl.ds(i * 8, 8), :]
                move = (pos - start) % 128
                v = pltpu.roll(v, move, 1) if move else v
                acc = v if acc is None else jnp.where(lane >= pos, v, acc)
        return acc

    def send_part(f):
        inner = pl.ds(0, BH)
        for k, (x, y) in enumerate(BAND):
            e = xs[x] + ys[y]
            packed[f][k, inner, :] = pack(f, e)
            if f == ORDER[3]:
                packed[f][k, pl.ds(BH, 8), :] = pack_sides(f, e)
            pltpu.make_async_remote_copy(
                src_ref=packed[f].at[k], dst_ref=landed[f].at[lon], send_sem=a2a_s.at[f], recv_sem=a2a_r.at[f],
                device_id={"lon": e, "lat": lat}).start()
        landed[f][lon, inner, :] = pack(f, lon)
        if f == ORDER[3]:
            landed[f][lon, pl.ds(BH, 8), :] = pack_sides(f, lon)

    def part_done(sem, f):
        most = landed[f].at[pl.ds(0, NLON - 1)]
        return pltpu.make_async_copy(most, most, sem.at[f])

    def stage_strips(f):
        for side, tile, start in ((0, 3, 92), (1, 0, 0)):
            acc = None
            for i in range(20):
                move = (4 * i - start) % 128
                v = al[f, pl.ds(i * 8, 8), pl.ds(tile * 128, 128)]
                v = pltpu.roll(v, move, 1) if move else v
                acc = v if acc is None else jnp.where(lane >= 4 * i, v, acc)
            strips_o[side, f] = acc

    def start_halo(h, f, n):
        fs = pl.ds(f, n)
        top, bottom, low, high = pl.ds(0, 8), pl.ds(152, 8), pl.ds(0, 128), pl.ds(384, 128)

        def copy(kind, src, dst, x, y):
            pltpu.make_async_remote_copy(
                src_ref=src, dst_ref=dst, send_sem=halo_s.at[h, kind], recv_sem=halo_r.at[h, kind],
                device_id={"lon": x, "lat": y}).start()
        copy(2, al.at[fs, top, low], corners_i.at[0, fs], west, north)
        copy(2, al.at[fs, top, high], corners_i.at[1, fs], east, north)
        copy(2, al.at[fs, bottom, low], corners_i.at[2, fs], west, south)
        copy(2, al.at[fs, bottom, high], corners_i.at[3, fs], east, south)
        copy(0, strips_o.at[0, fs], strips_i.at[0, fs], east, lat)
        copy(0, strips_o.at[1, fs], strips_i.at[1, fs], west, lat)
        copy(1, al.at[fs, top, :], rows_i.at[0, fs], lon, north)
        copy(1, al.at[fs, bottom, :], rows_i.at[1, fs], lon, south)

    def wait_halo(h, f, n):
        fs = pl.ds(f, n)
        for kind, ref in enumerate((strips_i, rows_i, corners_i)):
            for sem in (halo_s, halo_r):
                pltpu.make_async_copy(ref.at[:, fs], ref.at[:, fs], sem.at[h, kind]).wait()

    def unpack_halo(f):
        outer = pl.ds(384, 128)
        from_w, from_e = strips_i[0, f], strips_i[1, f]
        for i in range(20):
            rows = pl.ds(i * 8, 8)
            e = pltpu.roll(from_e, 96 - 4 * i, 1) if i != 24 else from_e
            w = pltpu.roll(from_w, 124 - 4 * i, 1)
            al[f, rows, outer] = jnp.where(lane < 96, al[f, rows, outer], jnp.where(lane < 112, e, w))
        last = jnp.where(sub_w < 4, rows_i[0, f], rows_i[1, f])
        e = pltpu.roll(jnp.where(sub < 4, corners_i[0, f], corners_i[2, f]), 96, 1)
        w = pltpu.roll(jnp.where(sub < 4, corners_i[1, f], corners_i[3, f]), 32, 1)
        al[f, pl.ds(160, 8), pl.ds(0, 384)] = last[:, :384]
        al[f, pl.ds(160, 8), outer] = jnp.where(lane < 96, last[:, 384:], jnp.where(lane < 112, e, w))

    def rows_of(i):
        return pl.ds(i * 8, 8) if isinstance(i, int) else pl.ds(pl.multiple_of(i * 8, 8), 8)

    def around(i):
        return rows_of(i), rows_of((i + TILES - 1) % TILES if isinstance(i, int) else lax.rem(i + TILES - 1, TILES)), rows_of((i + 1) % TILES if isinstance(i, int) else lax.rem(i + 1, TILES))

    def up(c, p):
        return pltpu.roll(jnp.where(sub_w == 7, p, c), 1, 0)

    def down(c, n):
        return pltpu.roll(jnp.where(sub_w == 0, n, c), 7, 0)

    def to_east(c):
        return pltpu.roll(c, 511, 1)

    def to_west(c):
        return pltpu.roll(c, 1, 1)

    get_kmt.wait()
    get_kappa.wait()

    def widen(i, _):
        rows = rows_of(i)
        for t in range(4):
            w = min(128, COLS - t * 128)
            at = pl.ds(t * 128, w)
            al[KMT, rows, at] = levels[rows, at].astype(f32)
            al[KAPPA, rows, at] = kap[0, rows, at]
            al[KAPPA + 1, rows, at] = kap[1, rows, at]
        return 0
    for i in range(20):
        widen(i, 0)
    for f in (4, 5, 6):
        stage_strips(f)
    spread(ORDER[0])
    to_scalars.wait()
    pl.semaphore_wait(barrier, len(EVERY))
    start_halo(4, 4, 3)
    send_part(ORDER[0])
    for f in ORDER[1:]:
        spread(f)
        if f == ORDER[1]:
            send_part(f)

    wait_halo(4, 4, 3)
    for f in (4, 5, 6):
        unpack_halo(f)
    inside_s = (lat != NLAT - 1).astype(f32)
    inside_n = (lat != 0).astype(f32)
    edge = al[KMT, pl.ds(160, 8), :]
    al[KMT, pl.ds(160, 8), :] = jnp.where(sub_w < 4, edge * inside_s, edge * inside_n)

    def faces(i, _):
        here, prev, after = around(i)
        kc = al[KMT, here, :]
        ku, kd, ke = up(kc, al[KMT, prev, :]), down(kc, al[KMT, after, :]), to_east(kc)
        ku, kd, ke = jnp.minimum(kc, ku), jnp.minimum(kc, kd), jnp.minimum(kc, ke)
        for l in range(2):
            c = al[KAPPA + l, here, :]
            face[3 * l, here, :] = jnp.where(ke > l, 0.5 * (c + to_east(c)), 0.0)
            face[3 * l + 1, here, :] = jnp.where(ku > l, 0.5 * (c + up(c, al[KAPPA + l, prev, :])), 0.0)
            face[3 * l + 2, here, :] = jnp.where(kd > l, 0.5 * (c + down(c, al[KAPPA + l, after, :])), 0.0)
        col[here, :] = (kc > 0).astype(f32)
        dep[here, :] = (kc > 0).astype(f32) + 1.5 * (kc > 1).astype(f32)
        return 0
    for i in range(TILES):
        faces(i, 0)

    def place(f):
        level = float(f % 2)

        def band(by, _):
            code = [table[0, 32 + by * BX + bx] for bx in range(BX)]
            src = [c >> 1 for c in code]
            second = [jnp.full((8, 128), c & 1, i32) == 1 for c in code]
            for i in range(5):
                rows_out = pl.ds(by * BH + i * 8, 8)
                v = []
                for bx in range(BX):
                    a = landed[f][src[bx], pl.ds(i * 8, 8), :]
                    o = (BW * bx) % 128
                    direct = pltpu.roll(a, o, 1) if o else a
                    crossed = pltpu.roll(a, (o + 64) % 128, 1)
                    v.append(jnp.where(second[bx], crossed, direct))
                for t, (x, y, z, p, q) in enumerate(((0, 1, 2, 60, 120), (2, 3, 4, 52, 112), (4, 5, 6, 44, 104), (6, 7, 7, 36, 128))):
                    at = pl.ds(t * 128, 128)
                    w = jnp.where(lane < p, v[x], jnp.where(lane < q, v[y], v[z]))
                    al[f, rows_out, at] = jnp.where(al[KMT, rows_out, at] > level, w, 0.0)
            return 0
        for by in range(BY):
            band(by, 0)

    def place_sides(f):
        level = float(f % 2)
        outer = pl.ds(384, 128)
        for by in range(BY):
            both = []
            for n in range(2):
                code = table[0, 64 + 4 * n + by]
                v = landed[f][code >> 1, pl.ds(BH, 8), :]
                both.append(jnp.where(jnp.full((8, 128), code & 1, i32) == 1, pltpu.roll(v, 124, 1), v))
            for i in range(5):
                rows = pl.ds(by * BH + i * 8, 8)
                e = pltpu.roll(both[0], 96 - 16 * i, 1)
                w = pltpu.roll(both[1], 116 - 16 * i, 1)
                v = jnp.where(al[KMT, rows, outer] > level, jnp.where(lane < 112, e, w), 0.0)
                al[f, rows, outer] = jnp.where(lane < 96, al[f, rows, outer], v)

    def row_copies(f):
        return [
            pltpu.make_async_remote_copy(
                src_ref=al.at[f, pl.ds(start, 8), :], dst_ref=rows_i.at[n, f], send_sem=halo_s.at[f, n], recv_sem=halo_r.at[f, n],
                device_id={"lon": lon, "lat": to})
            for n, (start, to) in enumerate(((0, north), (152, south)))
        ]

    def diffuse(f, first):
        t, l = divmod(f, 2)
        dz = 1.0 + 0.5 * l

        def tile(i, store):
            here, prev, after = around(i)
            c = al[f, here, :]
            fe = face[3 * l, here, :] * (to_east(c) - c)
            change = fe - to_west(fe)
            change = change + face[3 * l + 1, here, :] * (up(c, al[f, prev, :]) - c)
            change = change + face[3 * l + 2, here, :] * (down(c, al[f, after, :]) - c)
            v = jnp.where(al[KMT, here, :] > float(l), c + change, 0.0)
            if store:
                for p in range(4):
                    w = min(128, COLS - p * 128)
                    fresh_t[t, l, here, pl.ds(p * 128, w)] = v[:, p * 128:p * 128 + w]
            share = (dz * haline) * v if t else (-dz) * (thermal * v + cabbeling * v * v)
            vs[0, here, :] = share if first else vs[0, here, :] + share

        def several(j, _):
            for d in range(20):
                tile(20 * j + d, True)
            return 0
        several(0, 0)
        tile(TILES - 1, False)

    for n, f in enumerate(ORDER):
        part_done(a2a_r, f).wait()
        if n < 2:
            send_part(ORDER[n + 2])
        place(f)
        if n < 3:
            stage_strips(f)
            start_halo(f, f, 1)
        else:
            place_sides(f)
            last = row_copies(f)
            for c in last:
                c.start()
        if n >= 2:
            g = ORDER[n - 2]
            wait_halo(g, g, 1)
            unpack_halo(g)
            diffuse(g, n == 2)
    wait_halo(ORDER[2], ORDER[2], 1)
    unpack_halo(ORDER[2])
    diffuse(ORDER[2], False)
    for c in last:
        c.wait()
    f = ORDER[3]
    al[f, pl.ds(160, 8), :] = jnp.where(sub_w < 4, rows_i[0, f], rows_i[1, f])
    diffuse(f, False)
    result = pltpu.make_async_copy(fresh_t, out_t, out_sem.at[0])
    result.start()

    sums = []
    for order in range(3):
        def apply(i, acc, order=order, add=True):
            here, prev, after = around(i)
            c = vs[order, here, :]
            m = up(c, vs[order, prev, :]) + down(c, vs[order, after, :])
            q = c + 0.5 * m
            v = dep[here, :] * c - col[here, :] * (to_east(q) + to_west(q) + m)
            if order < 2:
                vs[order + 1, here, :] = v
            return (acc[0] + c * c, acc[1] + c * v) if add else acc

        def several(j, acc, apply=apply):
            for d in range(20):
                acc = apply(20 * j + d, acc)
            return acc
        zero = jnp.zeros((8, 512), f32)
        acc = several(0, (zero, zero))
        if order < 2:
            apply(TILES - 1, acc, add=False)
        sums += list(acc)

    powers = pltpu.make_async_copy(vs, out_v, out_sem.at[2])
    powers.start()
    tile = jnp.zeros((8, 128), f32)
    for k, s in enumerate(sums):
        s = s[:, :128] + s[:, 128:256] + s[:, 256:384] + jnp.where(lane < 96, s[:, 384:], 0.0)
        tile = jnp.where(sub == k, jnp.sum(s, axis=0, keepdims=True), tile)
    tile = jnp.where(sub == lane, jnp.sum(tile, axis=1, keepdims=True), 0.0)
    mine = jnp.sum(tile, axis=0, keepdims=True)
    part[...] = mine
    for k, (x, y, z, c) in enumerate(EVERY):
        pltpu.make_async_remote_copy(
            src_ref=part, dst_ref=gathered.at[k], send_sem=red_s, recv_sem=red_r,
            device_id={"lon": xs[x] + ys[y], "lat": zs[z] + cs[c]}).start()
    pltpu.make_async_copy(gathered, gathered, red_r).wait()
    total = mine + jnp.sum(gathered[...], axis=0)
    summed[...] = total
    sums_out = pltpu.make_async_copy(summed, out_n, out_sem.at[1])
    sums_out.start()

    for f in ORDER:
        part_done(a2a_s, f).wait()
    pltpu.make_async_copy(gathered, gathered, red_s).wait()
    result.wait()
    powers.wait()
    sums_out.wait()


def finish(made_t, made_v, made_n, out_t, out_s, fresh_t, vs, summed, stream, in_sem, out_sem):
    get_sums = pltpu.make_async_copy(made_n, summed, in_sem.at[4])
    get_powers = pltpu.make_async_copy(made_v, vs, in_sem.at[5])
    cells = [(t, l) for t in range(2) for l in range(2)]
    ins = [pltpu.make_async_copy(made_t.at[t, l], fresh_t.at[t, l], in_sem.at[2 * t + l]) for t, l in cells]
    outs = [pltpu.make_async_copy(fresh_t.at[t, l], out_t.at[t, l], out_sem.at[2 * t + l]) for t, l in cells]
    for load in [get_sums] + ins + [get_powers]:
        load.start()
    for load, store in zip(ins, outs):
        load.wait()
        store.start()
    get_sums.wait()
    total = summed[...]
    nu = [total[:, k:k + 1] for k in range(6)]

    def dot(a, b):
        total = None
        for i, x in enumerate(a):
            for j, y in enumerate(b):
                term = x * y * nu[i + j]
                total = term if total is None else total + term
        return total

    def image(a):
        return [SHIFT * a[0]] + [SHIFT * a[k] + a[k - 1] for k in range(1, len(a))] + [a[-1]]

    unit = jnp.ones((1, 1), f32)
    x = []
    res, direct, norm = [unit], [unit], nu[0]
    for k in range(3):
        img = image(direct)
        alpha = norm / dot(direct, img)
        x = [(x[n] + alpha * d) if n < len(x) else alpha * d for n, d in enumerate(direct)]
        if k < 2:
            res = [(res[n] - alpha * d) if n < len(res) else -alpha * d for n, d in enumerate(img)]
            later = dot(res, res)
            beta = later / norm
            direct = [(res[n] + beta * direct[n]) if n < len(direct) else res[n] for n in range(len(res))]
            norm = later

    c0, c1, c2 = (jnp.broadcast_to(v, (8, 128)) for v in x)
    get_powers.wait()
    for i in range(20):
        rows = pl.ds(i * 8, 8)
        for t in range(4):
            w = min(128, COLS - t * 128)
            at = pl.ds(t * 128, 128)
            v = c0 * vs[0, rows, at] + c1 * vs[1, rows, at] + c2 * vs[2, rows, at]
            stream[rows, pl.ds(t * 128, w)] = v[:, :w]
    final = pltpu.make_async_copy(stream, out_s, out_sem.at[4])
    final.start()
    for store in outs:
        store.wait()
    final.wait()


def body(checkpoint, slot_dest, kmt, kappa):
    sem = pltpu.SemaphoreType.DMA
    vm = pltpu.VMEM
    made = pl.pallas_call(
        kernel,
        out_shape=(
            jax.ShapeDtypeStruct((2, 2, ROWS, COLS), f32),
            jax.ShapeDtypeStruct((3, WIDE, 512), f32),
            jax.ShapeDtypeStruct((1, 128), f32),
        ),
        in_specs=[pl.BlockSpec(memory_space=pl.ANY)] * 4,
        out_specs=[pl.BlockSpec(memory_space=pl.ANY)] * 3,
        scratch_shapes=[
            vm((Q, 9600), f32),
            vm((1, NLON * Q), i32),
            vm((1, 128), i32),
            pltpu.SMEM((1, 128), i32),
            vm((4, Q, BH, 128), f32),
            *[vm((NLON - 1, BH, 128), f32)] * 3,
            vm((NLON - 1, BH + 8, 128), f32),
            *[vm((NLON, BH, 128), f32)] * 3,
            vm((NLON, BH + 8, 128), f32),
            vm((ROWS, COLS), i32),
            vm((2, ROWS, COLS), f32),
            vm((7, WIDE, 512), f32),
            vm((6, WIDE, 512), f32),
            vm((2, 7, 8, 128), f32),
            vm((2, 7, 8, 128), f32),
            vm((2, 7, 8, 512), f32),
            vm((4, 7, 8, 128), f32),
            vm((3, WIDE, 512), f32),
            vm((WIDE, 512), f32),
            vm((WIDE, 512), f32),
            vm((2, 2, ROWS, COLS), f32),
            vm((1, 128), f32),
            vm((1, 128), f32),
            vm((NLON * NLAT - 1, 1, 128), f32),
            sem((5,)),
            sem((3,)),
            sem((4,)),
            sem((4,)),
            sem((5, 3)),
            sem((5, 3)),
            sem,
            sem,
        ],
        compiler_params=pltpu.CompilerParams(collective_id=0, has_side_effects=True, vmem_limit_bytes=60 << 20),
    )(checkpoint[0], slot_dest, kmt, kappa)
    return pl.pallas_call(
        finish,
        out_shape=(jax.ShapeDtypeStruct((2, 2, ROWS, COLS), f32), jax.ShapeDtypeStruct((ROWS, COLS), f32)),
        in_specs=[pl.BlockSpec(memory_space=pl.ANY)] * 3,
        out_specs=[pl.BlockSpec(memory_space=pl.ANY)] * 2,
        scratch_shapes=[
            vm((2, 2, ROWS, COLS), f32),
            vm((3, WIDE, 512), f32),
            vm((1, 128), f32),
            vm((ROWS, COLS), f32),
            sem((6,)),
            sem((5,)),
        ],
        compiler_params=pltpu.CompilerParams(vmem_limit_bytes=60 << 20),
    )(*made)


def solution(mesh):
    placed = (P("lat", "lon", None), P("lat", None), P("lat", "lon"), P(None, "lat", "lon"))
    return jax.shard_map(
        body,
        mesh=mesh,
        in_specs=placed,
        out_specs=(P(None, None, "lat", "lon"), P("lat", "lon")),
        check_vma=False,
    )
```

```python
import jax
import jax.numpy as jnp
from jax import lax
from jax.experimental import pallas as pl
from jax.experimental.pallas import tpu as pltpu
from jax.sharding import PartitionSpec as P

BW = 60
BH = 40
BX = 8
BY = 4
Q = 32
ROWS = 160
COLS = 480
NLON = 16
NLAT = 8
SIDE = 4
TILES = 21
WIDE = TILES * 8
PART = BH * BW
SHIFT = 6.0
ORDER = (0, 2, 1, 3)
KAPPA, KMT = 4, 6

thermal = 0.25
haline = 0.75
cabbeling = 0.05

f32 = jnp.float32
i32 = jnp.int32


def hops(step):
    return (0, 1, 2, 1)[step]


BAND = [(1, 0), (2, 1), (0, 1), (1, 2), (3, 0), (2, 3), (0, 3), (3, 2), (1, 1), (2, 2), (3, 3), (2, 0), (1, 3), (0, 2), (3, 1)]
EVERY = sorted(
    [(x, y, z, c) for x in range(4) for y in range(4) for z in range(4) for c in range(2) if x or y or z or c],
    key=lambda k: -(hops(k[0]) + hops(k[1]) + hops(k[2])),
)


def kernel(ckpt, dest, kmt, kappa, out_t, out_v, out_n,
           blocks, slots, row, table, parted, packed0, packed1, packed2, packed3, landed0, landed1, landed2, landed3, levels, kap, al, face,
           strips_o, strips_i, rows_i, corners_i,
           vs, col, dep, fresh_t, part, summed, gathered,
           in_sem, out_sem, a2a_s, a2a_r, halo_s, halo_r, red_s, red_r):
    lon = lax.axis_index("lon")
    lat = lax.axis_index("lat")
    packed = (packed0, packed1, packed2, packed3)
    landed = (landed0, landed1, landed2, landed3)
    xs = [lax.rem(lon // SIDE + d, SIDE) * SIDE for d in range(4)]
    ys = [lax.rem(lax.rem(lon, SIDE) + d, SIDE) for d in range(4)]
    zs = [lax.rem(lat // 2 + d, 4) * 2 for d in range(4)]
    cs = [lax.rem(lat + d, 2) for d in range(2)]
    east, west = lax.rem(lon + 1, NLON), lax.rem(lon + NLON - 1, NLON)
    south, north = lax.rem(lat + 1, NLAT), lax.rem(lat + NLAT - 1, NLAT)

    get_slots = pltpu.make_async_copy(dest, slots, in_sem.at[0])
    get_blocks = pltpu.make_async_copy(ckpt, blocks, in_sem.at[1])
    get_kmt = pltpu.make_async_copy(kmt, levels, in_sem.at[2])
    get_kappa = pltpu.make_async_copy(kappa, kap, in_sem.at[3])
    for load in (get_slots, get_blocks, get_kmt, get_kappa):
        load.start()

    barrier = pltpu.get_barrier_semaphore()
    for x, y, z, c in EVERY:
        pl.semaphore_signal(barrier, inc=1, device_id={"lon": xs[x] + ys[y], "lat": zs[z] + cs[c]})

    lane = lax.broadcasted_iota(i32, (8, 128), 1)
    sub = lax.broadcasted_iota(i32, (8, 128), 0)
    lane32 = lax.broadcasted_iota(i32, (32, 128), 1)
    lane40 = lax.broadcasted_iota(i32, (BH, 128), 1)
    sub_w = lax.broadcasted_iota(i32, (8, 512), 0)

    get_slots.wait()
    dst = slots[...]
    owner = dst >> 5
    at = lax.broadcasted_iota(i32, (1, NLON * Q), 1)
    source, slot = at >> 5, at & 31
    line = lax.broadcasted_iota(i32, (8, NLON * Q), 0)
    count = (owner == jnp.where(line == 0, lon, jnp.where(line == 1, east, west))).astype(i32)
    slot_8 = lax.broadcasted_iota(i32, (8, NLON * Q), 1) & 31
    for d in (1, 2, 4, 8, 16):
        count = count + jnp.where(slot_8 >= d, pltpu.roll(count, d, 1), 0)
    code, code_e, code_w = (2 * source + jnp.clip(count[k:k + 1] - 1, 0, 1) for k in range(3))
    position = lax.broadcasted_iota(i32, (Q, NLON * Q), 0)
    found = jnp.max(jnp.where(dst == lon * Q + position, code, 0), axis=1, keepdims=True)
    beside = jnp.where(line < 4, east * Q + line * BX, west * Q + (line - 4) * BX + BX - 1)
    sides = jnp.max(jnp.where(dst == beside, jnp.where(line < 4, code_e, code_w), 0), axis=1, keepdims=True)
    to = jnp.where(source == lon, owner, -1) == lax.broadcasted_iota(i32, (NLON, NLON * Q), 0)
    one = jnp.min(jnp.where(to, slot, Q - 1), axis=1, keepdims=True)
    two = jnp.max(jnp.where(to, slot, 0), axis=1, keepdims=True)
    entries = jnp.concatenate([one, two, found, sides], axis=0)
    diagonal = lax.broadcasted_iota(i32, (72, 128), 0) == lax.broadcasted_iota(i32, (72, 128), 1)
    row[...] = jnp.sum(jnp.where(diagonal, entries, 0), axis=0, keepdims=True)
    to_scalars = pltpu.make_async_copy(row, table, in_sem.at[4])
    to_scalars.start()

    get_blocks.wait()

    def spread(f):
        flat = parted.at[f].reshape(Q * BH, 128)
        for r in range(BH):
            q, l = divmod(f * PART + r * BW, 128)
            a = blocks[:, pl.ds(q * 128, 128)]
            if l:
                a = pltpu.roll(a, 128 - l, 1)
            if l + BW > 128:
                b = blocks[:, pl.ds(q * 128 + 128, 128)]
                a = jnp.where(lane32 < 128 - l, a, pltpu.roll(b, 128 - l, 1))
            flat[pl.ds(r, Q, stride=BH), :] = a

    def pack(f, e):
        a = parted[f, table[0, e]]
        b = parted[f, table[0, NLON + e]]
        return jnp.where(lane40 < 64, a, pltpu.roll(b, 64, 1))

    def pack_sides(f, e):
        e_east, e_west = lax.rem(e + 1, NLON), lax.rem(e + NLON - 1, NLON)
        picks = [(table[0, e_east], 0), (table[0, NLON + e_east], 0), (table[0, e_west], 56), (table[0, NLON + e_west], 56)]
        acc = None
        for i in range(5):
            for n, (j, start) in enumerate(picks):
                pos = 16 * i + 4 * n
                v = parted[f, j, pl.ds(i * 8, 8), :]
                move = (pos - start) % 128
                v = pltpu.roll(v, move, 1) if move else v
                acc = v if acc is None else jnp.where(lane >= pos, v, acc)
        return acc

    def send_part(f):
        inner = pl.ds(0, BH)
        for k, (x, y) in enumerate(BAND):
            e = xs[x] + ys[y]
            packed[f][k, inner, :] = pack(f, e)
            if f == ORDER[3]:
                packed[f][k, pl.ds(BH, 8), :] = pack_sides(f, e)
            pltpu.make_async_remote_copy(
                src_ref=packed[f].at[k], dst_ref=landed[f].at[lon], send_sem=a2a_s.at[f], recv_sem=a2a_r.at[f],
                device_id={"lon": e, "lat": lat}).start()
        landed[f][lon, inner, :] = pack(f, lon)
        if f == ORDER[3]:
            landed[f][lon, pl.ds(BH, 8), :] = pack_sides(f, lon)

    def part_done(sem, f):
        most = landed[f].at[pl.ds(0, NLON - 1)]
        return pltpu.make_async_copy(most, most, sem.at[f])

    def stage_strips(f):
        for side, tile, start in ((0, 3, 92), (1, 0, 0)):
            acc = None
            for i in range(20):
                move = (4 * i - start) % 128
                v = al[f, pl.ds(i * 8, 8), pl.ds(tile * 128, 128)]
                v = pltpu.roll(v, move, 1) if move else v
                acc = v if acc is None else jnp.where(lane >= 4 * i, v, acc)
            strips_o[side, f] = acc

    def start_halo(h, f, n):
        fs = pl.ds(f, n)
        top, bottom, low, high = pl.ds(0, 8), pl.ds(152, 8), pl.ds(0, 128), pl.ds(384, 128)

        def copy(kind, src, dst, x, y):
            pltpu.make_async_remote_copy(
                src_ref=src, dst_ref=dst, send_sem=halo_s.at[h, kind], recv_sem=halo_r.at[h, kind],
                device_id={"lon": x, "lat": y}).start()
        copy(2, al.at[fs, top, low], corners_i.at[0, fs], west, north)
        copy(2, al.at[fs, top, high], corners_i.at[1, fs], east, north)
        copy(2, al.at[fs, bottom, low], corners_i.at[2, fs], west, south)
        copy(2, al.at[fs, bottom, high], corners_i.at[3, fs], east, south)
        copy(0, strips_o.at[0, fs], strips_i.at[0, fs], east, lat)
        copy(0, strips_o.at[1, fs], strips_i.at[1, fs], west, lat)
        copy(1, al.at[fs, top, :], rows_i.at[0, fs], lon, north)
        copy(1, al.at[fs, bottom, :], rows_i.at[1, fs], lon, south)

    def wait_halo(h, f, n):
        fs = pl.ds(f, n)
        for kind, ref in enumerate((strips_i, rows_i, corners_i)):
            for sem in (halo_s, halo_r):
                pltpu.make_async_copy(ref.at[:, fs], ref.at[:, fs], sem.at[h, kind]).wait()

    def unpack_halo(f):
        outer = pl.ds(384, 128)
        from_w, from_e = strips_i[0, f], strips_i[1, f]
        for i in range(20):
            rows = pl.ds(i * 8, 8)
            e = pltpu.roll(from_e, 96 - 4 * i, 1) if i != 24 else from_e
            w = pltpu.roll(from_w, 124 - 4 * i, 1)
            al[f, rows, outer] = jnp.where(lane < 96, al[f, rows, outer], jnp.where(lane < 112, e, w))
        last = jnp.where(sub_w < 4, rows_i[0, f], rows_i[1, f])
        e = pltpu.roll(jnp.where(sub < 4, corners_i[0, f], corners_i[2, f]), 96, 1)
        w = pltpu.roll(jnp.where(sub < 4, corners_i[1, f], corners_i[3, f]), 32, 1)
        al[f, pl.ds(160, 8), pl.ds(0, 384)] = last[:, :384]
        al[f, pl.ds(160, 8), outer] = jnp.where(lane < 96, last[:, 384:], jnp.where(lane < 112, e, w))

    def rows_of(i):
        return pl.ds(i * 8, 8) if isinstance(i, int) else pl.ds(pl.multiple_of(i * 8, 8), 8)

    def around(i):
        return rows_of(i), rows_of((i + TILES - 1) % TILES if isinstance(i, int) else lax.rem(i + TILES - 1, TILES)), rows_of((i + 1) % TILES if isinstance(i, int) else lax.rem(i + 1, TILES))

    def up(c, p):
        return pltpu.roll(jnp.where(sub_w == 7, p, c), 1, 0)

    def down(c, n):
        return pltpu.roll(jnp.where(sub_w == 0, n, c), 7, 0)

    def to_east(c):
        return pltpu.roll(c, 511, 1)

    def to_west(c):
        return pltpu.roll(c, 1, 1)

    get_kmt.wait()
    get_kappa.wait()

    def widen(i, _):
        rows = rows_of(i)
        for t in range(4):
            w = min(128, COLS - t * 128)
            at = pl.ds(t * 128, w)
            al[KMT, rows, at] = levels[rows, at].astype(f32)
            al[KAPPA, rows, at] = kap[0, rows, at]
            al[KAPPA + 1, rows, at] = kap[1, rows, at]
        return 0
    for i in range(20):
        widen(i, 0)
    for f in (4, 5, 6):
        stage_strips(f)
    spread(ORDER[0])
    to_scalars.wait()
    pl.semaphore_wait(barrier, len(EVERY))
    start_halo(4, 4, 3)
    send_part(ORDER[0])
    for f in ORDER[1:]:
        spread(f)
        if f == ORDER[1]:
            send_part(f)

    wait_halo(4, 4, 3)
    for f in (4, 5, 6):
        unpack_halo(f)
    inside_s = (lat != NLAT - 1).astype(f32)
    inside_n = (lat != 0).astype(f32)
    edge = al[KMT, pl.ds(160, 8), :]
    al[KMT, pl.ds(160, 8), :] = jnp.where(sub_w < 4, edge * inside_s, edge * inside_n)

    def faces(i, _):
        here, prev, after = around(i)
        kc = al[KMT, here, :]
        ku, kd, ke = up(kc, al[KMT, prev, :]), down(kc, al[KMT, after, :]), to_east(kc)
        ku, kd, ke = jnp.minimum(kc, ku), jnp.minimum(kc, kd), jnp.minimum(kc, ke)
        for l in range(2):
            c = al[KAPPA + l, here, :]
            face[3 * l, here, :] = jnp.where(ke > l, 0.5 * (c + to_east(c)), 0.0)
            face[3 * l + 1, here, :] = jnp.where(ku > l, 0.5 * (c + up(c, al[KAPPA + l, prev, :])), 0.0)
            face[3 * l + 2, here, :] = jnp.where(kd > l, 0.5 * (c + down(c, al[KAPPA + l, after, :])), 0.0)
        col[here, :] = (kc > 0).astype(f32)
        dep[here, :] = (kc > 0).astype(f32) + 1.5 * (kc > 1).astype(f32)
        return 0
    for i in range(TILES):
        faces(i, 0)

    def place(f, bands=range(BY)):
        level = float(f % 2)

        def band(by, _):
            code = [table[0, 32 + by * BX + bx] for bx in range(BX)]
            src = [c >> 1 for c in code]
            second = [jnp.full((8, 128), c & 1, i32) == 1 for c in code]
            for i in range(5):
                rows_out = pl.ds(by * BH + i * 8, 8)
                v = []
                for bx in range(BX):
                    a = landed[f][src[bx], pl.ds(i * 8, 8), :]
                    o = (BW * bx) % 128
                    direct = pltpu.roll(a, o, 1) if o else a
                    crossed = pltpu.roll(a, (o + 64) % 128, 1)
                    v.append(jnp.where(second[bx], crossed, direct))
                for t, (x, y, z, p, q) in enumerate(((0, 1, 2, 60, 120), (2, 3, 4, 52, 112), (4, 5, 6, 44, 104), (6, 7, 7, 36, 128))):
                    at = pl.ds(t * 128, 128)
                    w = jnp.where(lane < p, v[x], jnp.where(lane < q, v[y], v[z]))
                    al[f, rows_out, at] = jnp.where(al[KMT, rows_out, at] > level, w, 0.0)
            return 0
        for by in bands:
            band(by, 0)

    def place_sides(f, bands):
        level = float(f % 2)
        outer = pl.ds(384, 128)
        for by in bands:
            both = []
            for n in range(2):
                code = table[0, 64 + 4 * n + by]
                v = landed[f][code >> 1, pl.ds(BH, 8), :]
                both.append(jnp.where(jnp.full((8, 128), code & 1, i32) == 1, pltpu.roll(v, 124, 1), v))
            for i in range(5):
                rows = pl.ds(by * BH + i * 8, 8)
                e = pltpu.roll(both[0], 96 - 16 * i, 1)
                w = pltpu.roll(both[1], 116 - 16 * i, 1)
                v = jnp.where(al[KMT, rows, outer] > level, jnp.where(lane < 112, e, w), 0.0)
                al[f, rows, outer] = jnp.where(lane < 96, al[f, rows, outer], v)

    def row_copies(f):
        return [
            pltpu.make_async_remote_copy(
                src_ref=al.at[f, pl.ds(start, 8), :], dst_ref=rows_i.at[n, f], send_sem=halo_s.at[f, n], recv_sem=halo_r.at[f, n],
                device_id={"lon": lon, "lat": to})
            for n, (start, to) in enumerate(((0, north), (152, south)))
        ]

    def diffuse(f, first):
        t, l = divmod(f, 2)
        dz = 1.0 + 0.5 * l

        def tile(i, store):
            here, prev, after = around(i)
            c = al[f, here, :]
            fe = face[3 * l, here, :] * (to_east(c) - c)
            change = fe - to_west(fe)
            change = change + face[3 * l + 1, here, :] * (up(c, al[f, prev, :]) - c)
            change = change + face[3 * l + 2, here, :] * (down(c, al[f, after, :]) - c)
            v = jnp.where(al[KMT, here, :] > float(l), c + change, 0.0)
            if store:
                for p in range(4):
                    w = min(128, COLS - p * 128)
                    fresh_t[t, l, here, pl.ds(p * 128, w)] = v[:, p * 128:p * 128 + w]
            share = (dz * haline) * v if t else (-dz) * (thermal * v + cabbeling * v * v)
            vs[0, here, :] = share if first else vs[0, here, :] + share

        def several(j, _):
            for d in range(20):
                tile(20 * j + d, True)
            return 0
        several(0, 0)
        tile(TILES - 1, False)

    for n, f in enumerate(ORDER):
        part_done(a2a_r, f).wait()
        if n < 2:
            send_part(ORDER[n + 2])
        if n < 3:
            place(f)
        if n < 3:
            stage_strips(f)
            start_halo(f, f, 1)
        else:
            place(f, (0, BY - 1))
            place_sides(f, (0, BY - 1))
            last = row_copies(f)
            for c in last:
                c.start()
            place(f, range(1, BY - 1))
            place_sides(f, range(1, BY - 1))
        if n >= 2:
            g = ORDER[n - 2]
            wait_halo(g, g, 1)
            unpack_halo(g)
            diffuse(g, n == 2)
    wait_halo(ORDER[2], ORDER[2], 1)
    unpack_halo(ORDER[2])
    diffuse(ORDER[2], False)
    for c in last:
        c.wait()
    f = ORDER[3]
    al[f, pl.ds(160, 8), :] = jnp.where(sub_w < 4, rows_i[0, f], rows_i[1, f])
    diffuse(f, False)
    result = pltpu.make_async_copy(fresh_t, out_t, out_sem.at[0])
    result.start()

    sums = []
    for order in range(3):
        def apply(i, acc, order=order, add=True):
            here, prev, after = around(i)
            c = vs[order, here, :]
            m = up(c, vs[order, prev, :]) + down(c, vs[order, after, :])
            q = c + 0.5 * m
            v = dep[here, :] * c - col[here, :] * (to_east(q) + to_west(q) + m)
            if order < 2:
                vs[order + 1, here, :] = v
            return (acc[0] + c * c, acc[1] + c * v) if add else acc

        def several(j, acc, apply=apply):
            for d in range(20):
                acc = apply(20 * j + d, acc)
            return acc
        zero = jnp.zeros((8, 512), f32)
        acc = several(0, (zero, zero))
        if order < 2:
            apply(TILES - 1, acc, add=False)
        sums += list(acc)

    powers = pltpu.make_async_copy(vs, out_v, out_sem.at[2])
    powers.start()
    tile = jnp.zeros((8, 128), f32)
    for k, s in enumerate(sums):
        s = s[:, :128] + s[:, 128:256] + s[:, 256:384] + jnp.where(lane < 96, s[:, 384:], 0.0)
        tile = jnp.where(sub == k, jnp.sum(s, axis=0, keepdims=True), tile)
    tile = jnp.where(sub == lane, jnp.sum(tile, axis=1, keepdims=True), 0.0)
    mine = jnp.sum(tile, axis=0, keepdims=True)
    part[...] = mine
    for k, (x, y, z, c) in enumerate(EVERY):
        pltpu.make_async_remote_copy(
            src_ref=part, dst_ref=gathered.at[k], send_sem=red_s, recv_sem=red_r,
            device_id={"lon": xs[x] + ys[y], "lat": zs[z] + cs[c]}).start()
    pltpu.make_async_copy(gathered, gathered, red_r).wait()
    total = mine + jnp.sum(gathered[...], axis=0)
    summed[...] = total
    sums_out = pltpu.make_async_copy(summed, out_n, out_sem.at[1])
    sums_out.start()

    for f in ORDER:
        part_done(a2a_s, f).wait()
    pltpu.make_async_copy(gathered, gathered, red_s).wait()
    result.wait()
    powers.wait()
    sums_out.wait()


def finish(made_t, made_v, made_n, out_t, out_s, fresh_t, vs, summed, stream, in_sem, out_sem):
    get_sums = pltpu.make_async_copy(made_n, summed, in_sem.at[4])
    get_powers = pltpu.make_async_copy(made_v, vs, in_sem.at[5])
    cells = [(t, l) for t in range(2) for l in range(2)]
    ins = [pltpu.make_async_copy(made_t.at[t, l], fresh_t.at[t, l], in_sem.at[2 * t + l]) for t, l in cells]
    outs = [pltpu.make_async_copy(fresh_t.at[t, l], out_t.at[t, l], out_sem.at[2 * t + l]) for t, l in cells]
    for load in [get_sums] + ins + [get_powers]:
        load.start()
    for load, store in zip(ins, outs):
        load.wait()
        store.start()
    get_sums.wait()
    total = summed[...]
    nu = [total[:, k:k + 1] for k in range(6)]

    def dot(a, b):
        total = None
        for i, x in enumerate(a):
            for j, y in enumerate(b):
                term = x * y * nu[i + j]
                total = term if total is None else total + term
        return total

    def image(a):
        return [SHIFT * a[0]] + [SHIFT * a[k] + a[k - 1] for k in range(1, len(a))] + [a[-1]]

    unit = jnp.ones((1, 1), f32)
    x = []
    res, direct, norm = [unit], [unit], nu[0]
    for k in range(3):
        img = image(direct)
        alpha = norm / dot(direct, img)
        x = [(x[n] + alpha * d) if n < len(x) else alpha * d for n, d in enumerate(direct)]
        if k < 2:
            res = [(res[n] - alpha * d) if n < len(res) else -alpha * d for n, d in enumerate(img)]
            later = dot(res, res)
            beta = later / norm
            direct = [(res[n] + beta * direct[n]) if n < len(direct) else res[n] for n in range(len(res))]
            norm = later

    c0, c1, c2 = (jnp.broadcast_to(v, (8, 128)) for v in x)
    get_powers.wait()
    for i in range(20):
        rows = pl.ds(i * 8, 8)
        for t in range(4):
            w = min(128, COLS - t * 128)
            at = pl.ds(t * 128, 128)
            v = c0 * vs[0, rows, at] + c1 * vs[1, rows, at] + c2 * vs[2, rows, at]
            stream[rows, pl.ds(t * 128, w)] = v[:, :w]
    final = pltpu.make_async_copy(stream, out_s, out_sem.at[4])
    final.start()
    for store in outs:
        store.wait()
    final.wait()


def body(checkpoint, slot_dest, kmt, kappa):
    sem = pltpu.SemaphoreType.DMA
    vm = pltpu.VMEM
    made = pl.pallas_call(
        kernel,
        out_shape=(
            jax.ShapeDtypeStruct((2, 2, ROWS, COLS), f32),
            jax.ShapeDtypeStruct((3, WIDE, 512), f32),
            jax.ShapeDtypeStruct((1, 128), f32),
        ),
        in_specs=[pl.BlockSpec(memory_space=pl.ANY)] * 4,
        out_specs=[pl.BlockSpec(memory_space=pl.ANY)] * 3,
        scratch_shapes=[
            vm((Q, 9600), f32),
            vm((1, NLON * Q), i32),
            vm((1, 128), i32),
            pltpu.SMEM((1, 128), i32),
            vm((4, Q, BH, 128), f32),
            *[vm((NLON - 1, BH, 128), f32)] * 3,
            vm((NLON - 1, BH + 8, 128), f32),
            *[vm((NLON, BH, 128), f32)] * 3,
            vm((NLON, BH + 8, 128), f32),
            vm((ROWS, COLS), i32),
            vm((2, ROWS, COLS), f32),
            vm((7, WIDE, 512), f32),
            vm((6, WIDE, 512), f32),
            vm((2, 7, 8, 128), f32),
            vm((2, 7, 8, 128), f32),
            vm((2, 7, 8, 512), f32),
            vm((4, 7, 8, 128), f32),
            vm((3, WIDE, 512), f32),
            vm((WIDE, 512), f32),
            vm((WIDE, 512), f32),
            vm((2, 2, ROWS, COLS), f32),
            vm((1, 128), f32),
            vm((1, 128), f32),
            vm((NLON * NLAT - 1, 1, 128), f32),
            sem((5,)),
            sem((3,)),
            sem((4,)),
            sem((4,)),
            sem((5, 3)),
            sem((5, 3)),
            sem,
            sem,
        ],
        compiler_params=pltpu.CompilerParams(collective_id=0, has_side_effects=True, vmem_limit_bytes=60 << 20),
    )(checkpoint[0], slot_dest, kmt, kappa)
    return pl.pallas_call(
        finish,
        out_shape=(jax.ShapeDtypeStruct((2, 2, ROWS, COLS), f32), jax.ShapeDtypeStruct((ROWS, COLS), f32)),
        in_specs=[pl.BlockSpec(memory_space=pl.ANY)] * 3,
        out_specs=[pl.BlockSpec(memory_space=pl.ANY)] * 2,
        scratch_shapes=[
            vm((2, 2, ROWS, COLS), f32),
            vm((3, WIDE, 512), f32),
            vm((1, 128), f32),
            vm((ROWS, COLS), f32),
            sem((6,)),
            sem((5,)),
        ],
        compiler_params=pltpu.CompilerParams(vmem_limit_bytes=60 << 20),
    )(*made)


def solution(mesh):
    placed = (P("lat", "lon", None), P("lat", None), P("lat", "lon"), P(None, "lat", "lon"))
    return jax.shard_map(
        body,
        mesh=mesh,
        in_specs=placed,
        out_specs=(P(None, None, "lat", "lon"), P("lat", "lon")),
        check_vma=False,
    )
```
